32 devices in a mesh: groups: 2 (over x), req: 16 (over z, y, core).
Axes of the slice: x: 2, y: 2, z: 4, core: 2. Of those that a mesh axis runs over, the one named last changes fastest.
Arguments:
- queries: bfloat16 [2, 2048, 512], P(None, ('groups', 'req')), parts along dimension 1, may hold values from -40 to 40
- new_kv: bfloat16 [2, 2048, 128], P(None, ('groups', 'req')), parts along dimension 1, may hold values from -4 to 4
- cache: bfloat16 [2, 2048, 128, 128], P(None, ('groups', 'req')), parts along dimension 1, may hold values from -4 to 4
- lengths: int32 [2, 256], P(None, 'groups'), parts along dimension 1, may hold values from 2 to 128
- residual: bfloat16 [2, 256, 2880], P(None, ('groups', 'req')), parts along dimension 1, may hold values from -30 to 30
- o_proj: bfloat16 [4096, 2880], P('req'), may hold values from -1 to 1
- router: bfloat16 [2880, 16], replicated, may hold values from -0.109375 to 0.109375
- w_gate: bfloat16 [64, 2880, 360], P('req'), may hold values from -0.109375 to 0.109375
- w_up: bfloat16 [64, 2880, 360], P('req'), may hold values from -0.109375 to 0.109375
- w_down: bfloat16 [64, 360, 2880], P('req'), may hold values from -0.15625 to 0.15625
- routes: int32 [2, 256, 4], P(None, ('groups', 'req')), parts along dimension 1, may hold values from 0 to 15, all different within a row; in each aligned block of 8 rows (0 to 7, 8 to 15, ..., all dimensions but the last counted through in order) at most 4 rows name the same one
Outputs:
- attended: bfloat16 [2, 256, 2880], P(None, ('groups', 'req')), parts along dimension 1
- layer_out: bfloat16 [2, 256, 2880], P(None, ('groups', 'req')), parts along dimension 1
The draws below stay inside these ranges and needn't reach their ends.
There are 2 independent parts, one for each index of `groups`. The reference program is written for one: setup_inputs(seed, part) draws one part's arguments, and reference() takes and returns one part's arrays. A program takes and returns all parts, laid end to end along the dimension named above; an argument that names none is the same for every part. Nothing has to cross between parts.
Inputs may be any that keep to these rules, and one draw needn't show every extreme that they name: `routes`: each row names 4 different experts; of the 8 rows of one device of one micro-batch at most 4 name any one expert, and in every draw some expert is named by exactly 4 rows of some device.
All inputs are finite; a program needn't handle non-finite values.
Results may differ from the reference program's by a relative error of at most 0.0075.
Values may be sent and summed in bfloat16 or wider, within the bound.
No kernel may reach another device: no remote copies, remote signals or barrier semaphores. Data moves between devices by JAX's collectives and lax.ppermute only.
A program may use at most 128 MiB of HBM per device.

```python
import math
import jax
import jax.numpy as jnp
import numpy as np
from jax import lax

D = 2880
HD = 64
KVH = 8
QPK = 8
WIN = 128
EXPERTS = 16
FFW = 1440
SPLIT = 4
TOPK = 4
MB = 2
REQ_DEV = 8
FFS = 360
REQS = 128
CAP = 4


def draw_queries(key, part):
    shape_full = (MB, KVH * REQS, QPK * HD)
    values = jnp.clip(jax.random.normal(jax.random.fold_in(key, 1), shape_full, jnp.float32), -4.0, 4.0)
    return values.astype(jnp.bfloat16)


def draw_cache(key, part):
    shape_full = (MB, KVH * REQS, WIN, 2 * HD)
    values = jnp.clip(jax.random.normal(jax.random.fold_in(key, 2), shape_full, jnp.float32), -4.0, 4.0)
    return values.astype(jnp.bfloat16)


def draw_residual(key, part):
    shape_full = (MB, REQS, D)
    base = 0.5 * jnp.clip(jax.random.normal(jax.random.fold_in(key, 3), shape_full, jnp.float32), -3.0, 3.0)
    row_scale = jnp.exp(jax.random.uniform(jax.random.fold_in(key, 4), (MB, REQS, 1), jnp.float32, -1.15, 1.15))
    column_scale = jnp.exp(jax.random.uniform(jax.random.fold_in(key, 5), (1, 1, D), jnp.float32, -1.15, 1.15))
    return (base * row_scale * column_scale).astype(jnp.bfloat16)


def touch_ends(values, key, smallest, largest):
    place = [jax.random.randint(jax.random.fold_in(key, axis), (), 0, length) for axis, length in enumerate(values.shape)]
    main_axis = values.shape.index(max(values.shape))
    next_to = place[:main_axis] + [(place[main_axis] + 1) % values.shape[main_axis]] + place[main_axis + 1:]
    return values.at[tuple(place)].set(smallest).at[tuple(next_to)].set(largest)


def block_levels(rng, shape, pieces, low, largest):
    factor_of = 1.0
    for dim, shards_of in pieces:
        draws = jax.random.uniform(jax.random.fold_in(jax.random.fold_in(rng, 6), dim), (shards_of,), jnp.float32, low / len(pieces), largest / len(pieces))
        factor_of = factor_of * jnp.repeat(jnp.exp(draws), shape[dim] // shards_of).reshape((-1,) + (1,) * (len(shape) - 1 - dim))
    return factor_of


def deal_out(stream_key, own, number, rows, number_of, top, limit, skew):
    ranking = jax.random.permutation(stream_key, number_of)
    heavy_load, common = shares(number_of, rows * top, limit, skew, True), shares(number_of, rows * top, limit, skew, False)
    places = jnp.arange(number_of)

    def named(sizes, turn):
        used = int((sizes > 0).sum())
        fixed = max(1, used // 4)
        moved = fixed + (places - fixed + turn * (used - fixed)) % max(1, number_of - fixed)
        return jnp.zeros((number_of,), jnp.int32).at[ranking[jnp.where(places < fixed, places, moved)]].set(jnp.asarray(sizes, jnp.int32))

    sizes = jnp.where(number % 4 == 0, named(heavy_load, number // 4), named(common, number - number // 4 - 1))
    mixed = jax.random.permutation(jax.random.fold_in(own, 3), number_of)
    giver, receiver = mixed[0:number_of // 2 * 2:2], mixed[1:number_of // 2 * 2:2]
    slack = jnp.minimum(sizes[giver] - 1, limit - sizes[receiver]) // 2
    slack = jnp.where((giver == ranking[0]) | (receiver == ranking[0]) | (sizes[receiver] == 0), 0, jnp.maximum(slack, 0))
    moved = jax.random.randint(jax.random.fold_in(own, 4), (number_of // 2,), 0, 1 << 20) % (slack + 1)
    sizes = sizes.at[giver].add(-moved).at[receiver].add(moved)
    members = jnp.searchsorted(jnp.cumsum(sizes), jnp.arange(rows * top), side="right").astype(jnp.int32)
    grid = members.reshape(top, rows).T
    grid = grid[jax.random.permutation(jax.random.fold_in(own, 1), rows)]
    turn = jax.random.randint(jax.random.fold_in(own, 2), (rows, 1), 0, top)
    return jnp.take_along_axis(grid, (jnp.arange(top)[None, :] + turn) % top, axis=1)


def shares(number_of, total, most, lean, full):
    weights = [(1 << 20) // math.isqrt(grade ** lean) + 1 for grade in range(1, number_of + 1)]
    largest = most if full else min(most, max(-(-total // number_of), total * weights[0] // sum(weights)))
    least = 1 if total - largest >= number_of - 1 else 0
    given, spare = [largest] + [least] * (number_of - 1), total - largest - least * (number_of - 1)
    while spare > 0:
        movable = [i for i in range(1, number_of) if given[i] < largest] or [i for i in range(1, number_of) if given[i] < most]
        mass, remaining = sum([weights[i] for i in movable]), spare
        for i in movable:
            more = min(most - given[i], max(1, remaining * weights[i] // mass), spare)
            given[i] = given[i] + more
            spare = spare - more
    return np.array(given)


def bell_draw(own_key, dims, width, most, pieces=(), kind=jnp.bfloat16):
    values = jax.random.normal(own_key, dims, jnp.float32) * width
    if len(pieces) > 0:
        values = block_levels(own_key, dims, pieces, -0.22, 0.18) * values
    return jnp.clip(values, min=-most, max=most).astype(kind)


def setup_inputs(seed: int = 0, part: int = 0) -> dict:
    keys = jax.random.split(jax.random.key(seed), 12)
    part_splits = jax.random.split(jax.random.fold_in(keys[11], part), 12)
    queries = draw_queries(jax.random.fold_in(jax.random.fold_in(keys[11], part), 71), part)
    new_kv = bell_draw(part_splits[1], (MB, KVH * REQS, 2 * HD), 1.0, 4.0, ((1, 16),))
    cache = draw_cache(jax.random.fold_in(jax.random.fold_in(keys[11], part), 71), part)
    lengths = touch_ends(jax.random.randint(part_splits[3], (MB, REQS), 2, WIN + 1), jax.random.fold_in(part_splits[3], 1), 2, WIN).astype(jnp.int32)
    residual = draw_residual(jax.random.fold_in(jax.random.fold_in(keys[11], part), 71), part)
    o_proj = bell_draw(keys[5], (KVH * QPK * HD, D), 0.0625, 1.0, ((0, 16),))
    router = bell_draw(keys[6], (D, EXPERTS), D ** -0.5, 0.109375)
    w_gate = bell_draw(keys[7], (EXPERTS * SPLIT, D, FFS), D ** -0.5, 0.109375, ((0, 16),))
    w_up = bell_draw(keys[8], (EXPERTS * SPLIT, D, FFS), D ** -0.5, 0.109375, ((0, 16),))
    w_down = bell_draw(keys[9], (EXPERTS * SPLIT, FFS, D), FFW ** -0.5, 0.15625, ((0, 16),))
    routes_keys = jax.random.split(jax.random.fold_in(part_splits[10], 1), MB * REQS // REQ_DEV)
    routes_turns = jax.random.permutation(jax.random.fold_in(part_splits[10], 3), MB * REQS // REQ_DEV)
    routes = jax.vmap(lambda own, number: deal_out(jax.random.fold_in(part_splits[10], 2), own, number, REQ_DEV, EXPERTS, TOPK, CAP, 2))(routes_keys, routes_turns).reshape((MB, REQS, TOPK))
    return dict(queries=queries, new_kv=new_kv, cache=cache, lengths=lengths, residual=residual, o_proj=o_proj, router=router, w_gate=w_gate, w_up=w_up, w_down=w_down, routes=routes)


def attention_rows(query_rows, new_pair, cache_rows, live_count):
    row_total = query_rows.shape[0]
    query_heads = query_rows.reshape(row_total, QPK, HD).astype(jnp.float32)
    keys_cached = cache_rows[:, :, :HD].astype(jnp.float32)
    values_cached = cache_rows[:, :, HD:].astype(jnp.float32)
    key_fresh = new_pair[:, :HD].astype(jnp.float32)
    value_fresh = new_pair[:, HD:].astype(jnp.float32)
    factor = 1.0 / math.sqrt(HD)
    scores = jnp.einsum('rqd,rpd->rqp', query_heads, keys_cached) * factor
    own_score = jnp.einsum('rqd,rd->rq', query_heads, key_fresh) * factor
    live = jnp.arange(WIN)[None, None, :] < live_count[:, None, None]
    masked = jnp.where(live, scores, -jnp.inf)
    top_score = jnp.maximum(lax.optimization_barrier(jnp.max(masked, axis=2)), own_score)
    weight_cached = jnp.exp(masked - top_score[:, :, None])
    weight_own = jnp.exp(own_score - top_score)
    total = lax.optimization_barrier(jnp.sum(weight_cached, axis=2)) + weight_own
    prob_cached = lax.optimization_barrier((weight_cached / total[:, :, None]).astype(jnp.bfloat16))
    prob_own = lax.optimization_barrier((weight_own / total).astype(jnp.bfloat16))
    mixed = jnp.einsum('rqp,rpd->rqd', prob_cached.astype(jnp.float32), values_cached)
    mixed = mixed + prob_own.astype(jnp.float32)[:, :, None] * value_fresh[:, None, :]
    return mixed.astype(jnp.bfloat16).reshape(row_total, QPK * HD)

def expert_block(operands):
    rows_in, gate_full, up_full, down_full = operands
    gate_hidden = jnp.dot(rows_in, gate_full, preferred_element_type=jnp.float32)
    up_hidden = jnp.dot(rows_in, up_full, preferred_element_type=jnp.float32)
    active = ((up_hidden + 1.0) * gate_hidden * jax.nn.sigmoid(1.702 * gate_hidden)).astype(jnp.bfloat16)
    return jnp.dot(active, down_full, preferred_element_type=jnp.float32)

def reference(queries, new_kv, cache, lengths, residual, o_proj, router, w_gate, w_up, w_down, routes):
    request_count = residual.shape[1]
    block_count = request_count // REQ_DEV
    gate_full = w_gate.reshape(EXPERTS, SPLIT, D, FFS).transpose(0, 2, 1, 3).reshape(EXPERTS, D, SPLIT * FFS)
    up_full = w_up.reshape(EXPERTS, SPLIT, D, FFS).transpose(0, 2, 1, 3).reshape(EXPERTS, D, SPLIT * FFS)
    down_full = w_down.reshape(EXPERTS, SPLIT * FFS, D)
    attended_list = []
    layer_list = []
    for batch_index in range(MB):
        live_rows = jnp.tile(lengths[batch_index], KVH)
        mixed = attention_rows(queries[batch_index], new_kv[batch_index], cache[batch_index], live_rows)
        heads_all = mixed.reshape(KVH, request_count, QPK * HD).transpose(1, 0, 2).reshape(request_count, KVH * QPK * HD)
        attended = (residual[batch_index].astype(jnp.float32) + jnp.dot(heads_all, o_proj, preferred_element_type=jnp.float32)).astype(jnp.bfloat16)
        attended_wide = attended.astype(jnp.float32)
        normed = (attended_wide * lax.rsqrt(lax.optimization_barrier(jnp.mean(attended_wide * attended_wide, axis=1, keepdims=True)) + 1e-05)).astype(jnp.bfloat16)
        logits = jnp.dot(normed, router, preferred_element_type=jnp.float32)
        route_ids = routes[batch_index]
        chosen = jnp.take_along_axis(logits, route_ids, axis=1)
        gates = 1.0 / lax.optimization_barrier(jnp.sum(jnp.exp(chosen[:, None, :] - chosen[:, :, None]), axis=2))
        one_hot = (route_ids[:, :, None] == jnp.arange(EXPERTS, dtype=jnp.int32)[None, None, :]).astype(jnp.int32)
        by_block = one_hot.reshape(block_count, REQ_DEV * TOPK, EXPERTS)
        earlier = jnp.cumsum(by_block, axis=1) - by_block
        ranks = lax.optimization_barrier(jnp.sum(earlier * by_block, axis=2)).reshape(request_count, TOPK)
        block_of_row = (jnp.arange(request_count, dtype=jnp.int32) // REQ_DEV)[:, None]
        slot_index = (route_ids * (block_count * CAP) + block_of_row * CAP + ranks).astype(jnp.int32)
        buffer = jnp.zeros((EXPERTS * block_count * CAP, D), jnp.bfloat16)
        buffer = buffer.at[slot_index.reshape(-1)].set(jnp.repeat(normed, TOPK, axis=0))
        expert_rows = buffer.reshape(EXPERTS, block_count * CAP, D)
        produced = lax.map(expert_block, (expert_rows, gate_full, up_full, down_full))
        flat_out = produced.reshape(EXPERTS * block_count * CAP, D)
        picked = jnp.take(flat_out, slot_index, axis=0)
        mixture = lax.optimization_barrier(jnp.sum(gates[:, :, None] * picked, axis=1))
        layer = (attended_wide + mixture).astype(jnp.bfloat16)
        attended_list.append(attended)
        layer_list.append(layer)
    return (jnp.stack(attended_list), jnp.stack(layer_list))
```

```python
import math

import jax
import jax.numpy as jnp
from jax import lax
from jax.sharding import PartitionSpec as P

HD = 64
KVH = 8
QPK = 8
EXPERTS = 16
SPLIT = 4
REQ_DEV = 8


def plan(device_count):
    bits = device_count.bit_length() - 1
    stages = [(0, 1)] if bits else []
    bit = 1
    while bit < bits:
        width = min(2, bits - bit)
        stages.append((bit, width))
        bit += width
    masks = [0]
    for bit, width in stages:
        masks = [mask | (r << bit) for mask in masks for r in range(1 << width)]
    return stages, masks


def from_mask(value, mask):
    pairs = [(source, source ^ mask) for source in range(lax.axis_size("req"))]
    return lax.ppermute(value, "req", pairs)


def scatter_sum(parts, stages):
    for bit, width in stages:
        parts = parts.reshape((1 << width, -1) + parts.shape[1:])
        total = parts[0].astype(jnp.float32)
        for r in range(1, 1 << width):
            total = total + from_mask(parts[r].astype(jnp.bfloat16), r << bit).astype(jnp.float32)
        parts = total
    return parts[0]


def gather_rows(rows, stages):
    held = rows[None]
    for bit, width in reversed(stages):
        held = jnp.concatenate(
            [held] + [from_mask(held, r << bit) for r in range(1, 1 << width)], axis=0
        )
    return held


def attention_rows(query_rows, new_pair, cache_rows, live_count):
    row_total = query_rows.shape[0]
    window = cache_rows.shape[1]
    query_heads = query_rows.reshape(row_total, QPK, HD)
    factor = 1.0 / math.sqrt(HD)
    scores = (
        jnp.einsum(
            "rqd,rpd->rqp", query_heads, cache_rows[:, :, :HD], preferred_element_type=jnp.float32
        )
        * factor
    )
    own_score = (
        jnp.einsum("rqd,rd->rq", query_heads, new_pair[:, :HD], preferred_element_type=jnp.float32)
        * factor
    )
    live = jnp.arange(window)[None, None, :] < live_count[:, None, None]
    masked = jnp.where(live, scores, -jnp.inf)
    top_score = jnp.maximum(jnp.max(masked, axis=2), own_score)
    weight_cached = jnp.exp(masked - top_score[:, :, None])
    weight_own = jnp.exp(own_score - top_score)
    total = jnp.sum(weight_cached, axis=2) + weight_own
    prob_cached = (weight_cached / total[:, :, None]).astype(jnp.bfloat16)
    prob_own = (weight_own / total).astype(jnp.bfloat16)
    mixed = jnp.einsum(
        "rqp,rpd->rqd", prob_cached, cache_rows[:, :, HD:], preferred_element_type=jnp.float32
    )
    mixed = (
        mixed
        + prob_own.astype(jnp.float32)[:, :, None]
        * new_pair[:, HD:].astype(jnp.float32)[:, None, :]
    )
    return mixed.astype(jnp.bfloat16).reshape(row_total, QPK * HD)


def trade_heads(mixed, group_size, device_index):
    batch, rows, width = mixed.shape
    mine = device_index % group_size
    by_member = mixed.reshape(batch, rows, group_size, width // group_size)
    held = []
    for r in range(group_size):
        part = lax.dynamic_index_in_dim(by_member, mine ^ r, 2, keepdims=False)
        held.append(part if r == 0 else from_mask(part, r))
    held = jnp.stack(held)
    held = jnp.take(held, mine ^ jnp.arange(group_size), axis=0)
    return held.transpose(0, 2, 1, 3).reshape(group_size * rows, batch, width // group_size)


def shards(queries, new_kv, cache, lengths, residual, o_proj, router, w_gate, w_up, w_down, routes):
    device_count = lax.axis_size("req")
    device_index = lax.axis_index("req")
    stages, masks = plan(device_count)
    group_size = max(1, device_count // KVH)
    batch, local_rows = queries.shape[:2]
    width = residual.shape[2]
    block_rows = batch * REQ_DEV
    block_index = device_index % group_size
    local_lengths = lax.dynamic_slice_in_dim(lengths, block_index * local_rows, local_rows, 1)

    mixed = attention_rows(
        queries.reshape((-1,) + queries.shape[2:]),
        new_kv.reshape((-1,) + new_kv.shape[2:]),
        cache.reshape((-1,) + cache.shape[2:]),
        local_lengths.reshape(-1),
    ).reshape(batch, local_rows, QPK * HD)
    heads = trade_heads(mixed, group_size, device_index)
    heads = heads.reshape(device_count, REQ_DEV, batch, -1).transpose(0, 2, 1, 3)
    heads = jnp.take(heads, device_index ^ jnp.array(masks, jnp.int32), axis=0)
    parts = jnp.dot(
        heads.reshape(device_count * block_rows, -1), o_proj, preferred_element_type=jnp.float32
    ).reshape(device_count, block_rows, width)
    summed = scatter_sum(parts, stages)

    attended = (residual.reshape(block_rows, width).astype(jnp.float32) + summed).astype(
        jnp.bfloat16
    )
    attended_wide = attended.astype(jnp.float32)
    normed = (
        attended_wide
        * lax.rsqrt(jnp.mean(attended_wide * attended_wide, axis=1, keepdims=True) + 1e-05)
    ).astype(jnp.bfloat16)
    logits = jnp.dot(normed, router, preferred_element_type=jnp.float32)
    chosen_one = routes.reshape(block_rows, -1)[:, :, None] == jnp.arange(EXPERTS)[None, None, :]
    chosen = jnp.sum(jnp.where(chosen_one, logits[:, None, :], 0.0), axis=2)
    gates = 1.0 / jnp.sum(jnp.exp(chosen[:, None, :] - chosen[:, :, None]), axis=2)
    dense = jnp.sum(jnp.where(chosen_one, gates[:, :, None], 0.0), axis=1)
    high = lax.reduce_precision(dense, 8, 7)
    payload = jnp.concatenate(
        [normed, high.astype(jnp.bfloat16), (dense - high).astype(jnp.bfloat16)], axis=1
    )

    gathered = gather_rows(payload, stages).reshape(device_count * block_rows, -1)
    rows_in = gathered[:, :width]
    tail = gathered[:, width:].astype(jnp.float32)
    all_gates = tail[:, :EXPERTS] + tail[:, EXPERTS:]
    local_entries = w_gate.shape[0]
    partial = 0.0
    for entry in range(local_entries):
        expert = (device_index * local_entries + entry) // SPLIT
        gate_hidden = jnp.dot(rows_in, w_gate[entry], preferred_element_type=jnp.float32)
        up_hidden = jnp.dot(rows_in, w_up[entry], preferred_element_type=jnp.float32)
        active = ((up_hidden + 1.0) * gate_hidden * jax.nn.sigmoid(1.702 * gate_hidden)).astype(
            jnp.bfloat16
        )
        out = jnp.dot(active, w_down[entry], preferred_element_type=jnp.float32)
        partial = partial + out * lax.dynamic_slice_in_dim(all_gates, expert, 1, 1)
    mixture = scatter_sum(partial.reshape(device_count, block_rows, width), stages)
    layer = (attended_wide + mixture).astype(jnp.bfloat16)
    return attended.reshape(residual.shape), layer.reshape(residual.shape)


def solution(mesh):
    placed = (
        P(None, ("groups", "req"), None),
        P(None, ("groups", "req"), None),
        P(None, ("groups", "req"), None, None),
        P(None, "groups"),
        P(None, ("groups", "req"), None),
        P("req", None),
        P(),
        P("req", None, None),
        P("req", None, None),
        P("req", None, None),
        P(None, ("groups", "req"), None),
    )
    return jax.shard_map(
        shards,
        mesh=mesh,
        in_specs=placed,
        out_specs=(P(None, ("groups", "req"), None), P(None, ("groups", "req"), None)),
        check_vma=False,
    )
```

```python
import functools
import math

import jax
import jax.numpy as jnp
from jax import lax
from jax.experimental import pallas as pl
from jax.experimental.pallas import tpu as pltpu
from jax.sharding import PartitionSpec as P

HD = 64
KVH = 8
QPK = 8
EXPERTS = 16
SPLIT = 4
REQ_DEV = 8
CHUNK = 128
ROWS_LAST = (((1,), (1,)), ((), ()))


def plan(device_count):
    bits = device_count.bit_length() - 1
    stages = [(0, 1)] if bits else []
    bit = 1
    while bit < bits:
        width = min(2, bits - bit)
        stages.append((bit, width))
        bit += width
    masks = [0]
    for bit, width in stages:
        masks = [mask | (r << bit) for mask in masks for r in range(1 << width)]
    return stages, masks


def from_mask(value, mask):
    pairs = [(source, source ^ mask) for source in range(lax.axis_size("req"))]
    return lax.ppermute(value, "req", pairs)


def scatter_sum(keep, send, stages):
    block_rows, width = keep.shape[0], keep.shape[1]
    total = keep.astype(jnp.float32) + from_mask(send, 1).astype(jnp.float32)
    for bit, bits in stages[1:]:
        size = total.shape[0] >> bits
        pieces = [total[r * size : (r + 1) * size] for r in range(1 << bits)]
        total = pieces[0]
        for r in range(1, 1 << bits):
            moved = from_mask(pieces[r].astype(jnp.bfloat16), r << bit)
            total = total + moved.astype(jnp.float32)
    return total


def gather_rows(rows, stages):
    pieces = [rows]
    for bit, bits in reversed(stages):
        if bit:
            held = jnp.concatenate(pieces, axis=0) if len(pieces) > 1 else pieces[0]
            pieces = [held] + [from_mask(held, r << bit) for r in range(1, 1 << bits)]
        else:
            pieces = pieces + [from_mask(piece, 1) for piece in pieces]
    return pieces


def attention_kernel(
    group, blocks, lengths, place, q_ref, kv_ref, cache_ref, *refs
):
    outs = refs[:group]
    query, scores, mixed = refs[group:]
    rows, window, pair = cache_ref.shape
    batch, block = pl.program_id(0), pl.program_id(1)
    low = lax.broadcasted_iota(jnp.int32, (rows, pair), 1) < HD
    for h in range(QPK):
        tile = q_ref[:, (h // 2) * pair : (h // 2 + 1) * pair].astype(jnp.float32)
        tile = tile * (1.0 / math.sqrt(HD))
        if h % 2:
            tile = pltpu.roll(tile, HD, 1)
        query[pl.ds(h, rows, stride=QPK), :] = jnp.where(low, tile, 0.0)
    fresh = kv_ref[...].astype(jnp.float32)
    fresh = jnp.broadcast_to(fresh[:, None, :], (rows, QPK, pair)).reshape(rows * QPK, pair)
    own = jnp.sum(query[...] * fresh, axis=1, keepdims=True)
    position = lax.broadcasted_iota(jnp.int32, (QPK, window), 1)
    first = place[0] * (rows * blocks) + block * rows
    for r in range(rows):
        part = slice(r * QPK, (r + 1) * QPK)
        found = lax.dot_general(
            query[part, :].astype(jnp.bfloat16),
            cache_ref[r],
            ROWS_LAST,
            preferred_element_type=jnp.float32,
        )
        scores[part, :] = jnp.where(position < lengths[batch, first + r], found, -jnp.inf)
    top = jnp.maximum(jnp.max(scores[...], axis=1, keepdims=True), own)
    weight = jnp.exp(scores[...] - top)
    weight_own = jnp.exp(own - top)
    total = jnp.sum(weight, axis=1, keepdims=True) + weight_own
    scores[...] = weight / total
    prob_own = (weight_own / total).astype(jnp.bfloat16).astype(jnp.float32)
    for r in range(rows):
        part = slice(r * QPK, (r + 1) * QPK)
        mixed[part, :] = jnp.dot(
            scores[part, :].astype(jnp.bfloat16), cache_ref[r], preferred_element_type=jnp.float32
        )
    mixed[...] = mixed[...] + prob_own * fresh
    heads = QPK // group
    for r in range(group):
        start = (place[0] ^ r) * heads
        for j in range(0, heads, 2):
            left = pltpu.roll(mixed[pl.ds(start + j, rows, stride=QPK), :], HD, 1)
            if heads == 1:
                outs[r][...] = left[:, :HD].astype(jnp.bfloat16)
            else:
                right = mixed[pl.ds(start + j + 1, rows, stride=QPK), :]
                outs[r][:, j * HD : (j + 2) * HD] = jnp.where(low, left, right).astype(
                    jnp.bfloat16
                )


def attention(lengths, place, queries, new_kv, cache, group, block=32):
    batch, rows, window, pair = cache.shape
    block = min(block, rows)
    width = QPK // group * HD
    return pl.pallas_call(
        functools.partial(attention_kernel, group, rows // block),
        out_shape=[jax.ShapeDtypeStruct((batch, rows, width), jnp.bfloat16)] * group,
        grid_spec=pltpu.PrefetchScalarGridSpec(
            num_scalar_prefetch=2,
            grid=(batch, rows // block),
            in_specs=[
                pl.BlockSpec((None, block, QPK * HD), lambda m, i, *_: (m, i, 0)),
                pl.BlockSpec((None, block, pair), lambda m, i, *_: (m, i, 0)),
                pl.BlockSpec((None, block, window, pair), lambda m, i, *_: (m, i, 0, 0)),
            ],
            out_specs=[pl.BlockSpec((None, block, width), lambda m, i, *_: (m, i, 0))] * group,
            scratch_shapes=[
                pltpu.VMEM((block * QPK, pair), jnp.float32),
                pltpu.VMEM((block * QPK, window), jnp.float32),
                pltpu.VMEM((block * QPK, pair), jnp.float32),
            ],
        ),
        compiler_params=pltpu.CompilerParams(vmem_limit_bytes=60 << 20),
        name="attention",
    )(lengths, place, queries, new_kv, cache)


def project_kernel(group, masks, me_ref, *refs):
    held = refs[:group]
    weight, keep, send, wide, rows = refs[group:]
    batch, members, width = held[0].shape
    for r in range(group):
        wide[r] = held[r][...].astype(jnp.float32)
    me = me_ref[0]
    per_member = members // REQ_DEV
    for p, mask in enumerate(masks):
        block = me ^ mask
        member = (block // per_member) ^ (me % group)
        start = pl.multiple_of((block % per_member) * REQ_DEV, REQ_DEV)
        for m in range(batch):
            at = (p * batch + m) * REQ_DEV
            rows[at : at + REQ_DEV, :] = wide[member, m, pl.ds(start, REQ_DEV), :]
    half = keep.shape[0]
    send[...] = lax.dot_general(
        rows[half:, :].astype(jnp.bfloat16),
        weight[...],
        ROWS_LAST,
        preferred_element_type=jnp.float32,
    ).astype(jnp.bfloat16)
    keep[...] = lax.dot_general(
        rows[:half, :].astype(jnp.bfloat16),
        weight[...],
        ROWS_LAST,
        preferred_element_type=jnp.float32,
    )


def project(me, held, weight, masks):
    batch, members, width = held[0].shape
    group = len(held)
    count = len(masks) * batch * REQ_DEV
    whole = pl.BlockSpec(memory_space=pltpu.VMEM)
    return pl.pallas_call(
        functools.partial(project_kernel, group, masks),
        out_shape=[
            jax.ShapeDtypeStruct((count // 2, weight.shape[0]), jnp.float32),
            jax.ShapeDtypeStruct((count // 2, weight.shape[0]), jnp.bfloat16),
        ],
        in_specs=[pl.BlockSpec(memory_space=pltpu.SMEM)] + [whole] * (group + 1),
        out_specs=[whole] * 2,
        scratch_shapes=[
            pltpu.VMEM((group,) + held[0].shape, jnp.float32),
            pltpu.VMEM((count, width), jnp.float32),
        ],
        compiler_params=pltpu.CompilerParams(vmem_limit_bytes=32 << 20),
        name="project",
    )(me, *held, weight)


def expert_kernel(count, ahead, me_ref, *refs):
    pieces = refs[:count]
    sources = refs[count : count + 3]
    keep, send = refs[count + 3 : count + 5]
    rows, gates, ups, downs, active, total, done = refs[count + 5 :]
    entries, hidden, width = sources[0].shape
    order = [(k, e) for e in range(entries) for k in (0, 1)] + [(2, e) for e in range(entries)]
    stores = (gates, ups, downs)
    parts = pl.cdiv(hidden, CHUNK)
    copies = []
    for k, e in order:
        for s in range(parts):
            some = pl.ds(s * CHUNK, min(CHUNK, hidden - s * CHUNK))
            copies.append(
                pltpu.make_async_copy(
                    sources[k].at[e, some], stores[k].at[e, some], done.at[k, e, s]
                )
            )
    state = [0, 0]

    def issue():
        if state[0] < len(copies):
            copies[state[0]].start()
            state[0] += 1

    def finish():
        for _ in range(parts):
            copies[state[1]].wait()
            state[1] += 1
            issue()

    for _ in range(ahead):
        issue()
    at = 0
    for piece in pieces:
        rows[at : at + piece.shape[0], :] = piece[...]
        at += piece.shape[0]
    base = width // 128 * 128
    tail = rows[:, base:].astype(jnp.float32)
    lane = lax.broadcasted_iota(jnp.int32, tail.shape, 1) - (width - base)
    for e in range(entries):
        finish()
        gate = lax.dot_general(
            rows[:, :width], gates[e], ROWS_LAST, preferred_element_type=jnp.float32
        )
        finish()
        up = lax.dot_general(
            rows[:, :width], ups[e], ROWS_LAST, preferred_element_type=jnp.float32
        )
        active[e] = ((up + 1.0) * gate * jax.nn.sigmoid(1.702 * gate)).astype(jnp.bfloat16)
    half = keep.shape[0]
    local = max(1, entries // SPLIT)
    for e in range(entries):
        finish()
        out = jnp.dot(active[e], downs[e], preferred_element_type=jnp.float32)
        if e % SPLIT:
            out = out + total[...]
        if e + 1 < entries and (e + 1) % SPLIT:
            total[...] = out
            continue
        expert = me_ref[0] * entries // SPLIT + e // SPLIT
        picked = (lane == expert) | (lane == expert + EXPERTS)
        out = out * jnp.sum(jnp.where(picked, tail, 0.0), axis=1, keepdims=True)
        if e // SPLIT:
            keep[...] += out[:half]
            send[...] = (send[...].astype(jnp.float32) + out[half:]).astype(jnp.bfloat16)
        else:
            keep[...] = out[:half]
            send[...] = out[half:].astype(jnp.bfloat16)


def expert_sums(me, pieces, w_gate, w_up, w_down, ahead=9):
    entries, hidden, width = w_gate.shape
    count = sum(piece.shape[0] for piece in pieces)
    whole = pl.BlockSpec(memory_space=pltpu.VMEM)
    outside = pl.BlockSpec(memory_space=pl.ANY)
    parts = pl.cdiv(hidden, CHUNK)
    return pl.pallas_call(
        functools.partial(expert_kernel, len(pieces), ahead),
        out_shape=[
            jax.ShapeDtypeStruct((count // 2, width), jnp.float32),
            jax.ShapeDtypeStruct((count // 2, width), jnp.bfloat16),
        ],
        in_specs=[pl.BlockSpec(memory_space=pltpu.SMEM)]
        + [whole] * len(pieces)
        + [outside] * 3,
        out_specs=[whole] * 2,
        scratch_shapes=[
            pltpu.VMEM((count, pieces[0].shape[1]), jnp.bfloat16),
            pltpu.VMEM(w_gate.shape, jnp.bfloat16),
            pltpu.VMEM(w_up.shape, jnp.bfloat16),
            pltpu.VMEM(w_down.shape, jnp.bfloat16),
            pltpu.VMEM((entries, count, hidden), jnp.bfloat16),
            pltpu.VMEM((count, width), jnp.float32),
            pltpu.SemaphoreType.DMA((3, entries, parts)),
        ],
        compiler_params=pltpu.CompilerParams(vmem_limit_bytes=56 << 20),
        name="experts",
    )(me, *pieces, w_gate, w_up, w_down)


def shards(queries, new_kv, cache, lengths, residual, o_proj, router, w_gate, w_up, w_down, routes):
    device_count = lax.axis_size("req")
    device_index = lax.axis_index("req")
    stages, masks = plan(device_count)
    group_size = max(1, device_count // KVH)
    width = residual.shape[2]
    block_rows = residual.shape[0] * residual.shape[1]
    me = device_index.astype(jnp.int32)[None]

    held = attention(lengths, me % group_size, queries, new_kv, cache, group_size)
    held = [held[0]] + [from_mask(held[r], r) for r in range(1, group_size)]
    summed = scatter_sum(*project(me, held, o_proj.T, masks), stages)

    attended = (residual.reshape(block_rows, width).astype(jnp.float32) + summed).astype(
        jnp.bfloat16
    )
    attended_wide = attended.astype(jnp.float32)
    normed = (
        attended_wide
        * lax.rsqrt(jnp.mean(attended_wide * attended_wide, axis=1, keepdims=True) + 1e-05)
    ).astype(jnp.bfloat16)
    logits = jnp.dot(normed, router, preferred_element_type=jnp.float32)
    chosen_one = routes.reshape(block_rows, -1)[:, :, None] == jnp.arange(EXPERTS)[None, None, :]
    chosen = jnp.sum(jnp.where(chosen_one, logits[:, None, :], 0.0), axis=2)
    gates = 1.0 / jnp.sum(jnp.exp(chosen[:, None, :] - chosen[:, :, None]), axis=2)
    dense = jnp.sum(jnp.where(chosen_one, gates[:, :, None], 0.0), axis=1)
    high = lax.reduce_precision(dense, 8, 7)
    payload = jnp.concatenate(
        [normed, high.astype(jnp.bfloat16), (dense - high).astype(jnp.bfloat16)], axis=1
    )

    pieces = gather_rows(payload, stages)
    mixture = scatter_sum(
        *expert_sums(me, pieces, w_gate.swapaxes(1, 2), w_up.swapaxes(1, 2), w_down), stages
    )
    layer = (attended_wide + mixture).astype(jnp.bfloat16)
    return attended.reshape(residual.shape), layer.reshape(residual.shape)


def solution(mesh):
    placed = (
        P(None, ("groups", "req"), None),
        P(None, ("groups", "req"), None),
        P(None, ("groups", "req"), None, None),
        P(None, "groups"),
        P(None, ("groups", "req"), None),
        P("req", None),
        P(),
        P("req", None, None),
        P("req", None, None),
        P("req", None, None),
        P(None, ("groups", "req"), None),
    )
    return jax.shard_map(
        shards,
        mesh=mesh,
        in_specs=placed,
        out_specs=(P(None, ("groups", "req"), None), P(None, ("groups", "req"), None)),
        check_vma=False,
    )
```

```python
import functools
import math

import jax
import jax.numpy as jnp
from jax import lax
from jax.experimental import pallas as pl
from jax.experimental.pallas import tpu as pltpu
from jax.sharding import PartitionSpec as P

HD = 64
KVH = 8
QPK = 8
EXPERTS = 16
SPLIT = 4
REQ_DEV = 8
TILE = 256
LIMIT = 16 << 20
ROWS_LAST = (((1,), (1,)), ((), ()))


def plan(device_count):
    bits = device_count.bit_length() - 1
    stages = [(0, 1)] if bits else []
    bit = 1
    while bit < bits:
        width = min(2, bits - bit)
        stages.append((bit, width))
        bit += width
    masks = [0]
    for bit, width in stages:
        masks = [mask | (r << bit) for mask in masks for r in range(1 << width)]
    return stages, masks


def from_mask(value, mask):
    pairs = [(source, source ^ mask) for source in range(lax.axis_size("req"))]
    return lax.ppermute(value, "req", pairs)


def scatter_sum(keep, send, stages):
    width = keep.shape[1]
    total = keep + from_mask(send, 1)[:, :width].astype(jnp.float32)
    for bit, bits in stages[1:]:
        size = total.shape[0] >> bits
        pieces = [total[r * size : (r + 1) * size] for r in range(1 << bits)]
        total = pieces[0]
        for r in range(1, 1 << bits):
            moved = from_mask(pieces[r].astype(jnp.bfloat16), r << bit)
            total = total + moved.astype(jnp.float32)
    return total


def gather_rows(rows, stages):
    pieces = [rows]
    for bit, bits in reversed(stages):
        if bit:
            held = jnp.concatenate(pieces, axis=0) if len(pieces) > 1 else pieces[0]
            pieces = [held] + [from_mask(held, r << bit) for r in range(1, 1 << bits)]
        else:
            pieces = pieces + [from_mask(piece, 1) for piece in pieces]
    return pieces


def attention_kernel(
    group, blocks, lengths, place, q_ref, kv_ref, cache_ref, *refs
):
    outs = refs[:group]
    query, scores, mixed = refs[group:]
    rows, window, pair = cache_ref.shape
    batch, block = pl.program_id(0), pl.program_id(1)
    low = lax.broadcasted_iota(jnp.int32, (rows, pair), 1) < HD
    for h in range(QPK):
        tile = q_ref[:, (h // 2) * pair : (h // 2 + 1) * pair].astype(jnp.float32)
        tile = tile * (1.0 / math.sqrt(HD))
        if h % 2:
            tile = pltpu.roll(tile, HD, 1)
        query[pl.ds(h, rows, stride=QPK), :] = jnp.where(low, tile, 0.0)
    fresh = kv_ref[...].astype(jnp.float32)
    fresh = jnp.broadcast_to(fresh[:, None, :], (rows, QPK, pair)).reshape(rows * QPK, pair)
    own = jnp.sum(query[...] * fresh, axis=1, keepdims=True)
    position = lax.broadcasted_iota(jnp.int32, (QPK, window), 1)
    first = place[0] * (rows * blocks) + block * rows
    for r in range(rows):
        part = slice(r * QPK, (r + 1) * QPK)
        found = lax.dot_general(
            query[part, :].astype(jnp.bfloat16),
            cache_ref[r],
            ROWS_LAST,
            preferred_element_type=jnp.float32,
        )
        scores[part, :] = jnp.where(position < lengths[batch, first + r], found, -jnp.inf)
    top = jnp.maximum(jnp.max(scores[...], axis=1, keepdims=True), own)
    weight = jnp.exp(scores[...] - top)
    weight_own = jnp.exp(own - top)
    total = jnp.sum(weight, axis=1, keepdims=True) + weight_own
    scores[...] = weight / total
    prob_own = (weight_own / total).astype(jnp.bfloat16).astype(jnp.float32)
    for r in range(rows):
        part = slice(r * QPK, (r + 1) * QPK)
        mixed[part, :] = jnp.dot(
            scores[part, :].astype(jnp.bfloat16), cache_ref[r], preferred_element_type=jnp.float32
        )
    mixed[...] = mixed[...] + prob_own * fresh
    heads = QPK // group
    for r in range(group):
        start = (place[0] ^ r) * heads
        for j in range(0, heads, 2):
            left = pltpu.roll(mixed[pl.ds(start + j, rows, stride=QPK), :], HD, 1)
            if heads == 1:
                outs[r][...] = left[:, :HD].astype(jnp.bfloat16)
            else:
                right = mixed[pl.ds(start + j + 1, rows, stride=QPK), :]
                outs[r][:, j * HD : (j + 2) * HD] = jnp.where(low, left, right).astype(
                    jnp.bfloat16
                )


def attention(lengths, place, queries, new_kv, cache, group, block=32):
    batch, rows, window, pair = cache.shape
    block = min(block, rows)
    width = QPK // group * HD
    return pl.pallas_call(
        functools.partial(attention_kernel, group, rows // block),
        out_shape=[jax.ShapeDtypeStruct((batch, rows, width), jnp.bfloat16)] * group,
        grid_spec=pltpu.PrefetchScalarGridSpec(
            num_scalar_prefetch=2,
            grid=(batch, rows // block),
            in_specs=[
                pl.BlockSpec((None, block, QPK * HD), lambda m, i, *_: (m, i, 0)),
                pl.BlockSpec((None, block, pair), lambda m, i, *_: (m, i, 0)),
                pl.BlockSpec((None, block, window, pair), lambda m, i, *_: (m, i, 0, 0)),
            ],
            out_specs=[pl.BlockSpec((None, block, width), lambda m, i, *_: (m, i, 0))] * group,
            scratch_shapes=[
                pltpu.VMEM((block * QPK, pair), jnp.float32),
                pltpu.VMEM((block * QPK, window), jnp.float32),
                pltpu.VMEM((block * QPK, pair), jnp.float32),
            ],
        ),
        compiler_params=pltpu.CompilerParams(vmem_limit_bytes=61 << 20),
        name="attention",
    )(lengths, place, queries, new_kv, cache)


def project_kernel(group, masks, me_ref, *refs):
    held = refs[:group]
    weight, keep, send, wide, rows = refs[group:]
    batch, members, width = held[0].shape
    for r in range(group):
        wide[r] = held[r][...].astype(jnp.float32)
    me = me_ref[0]
    per_member = members // REQ_DEV
    for p, mask in enumerate(masks):
        block = me ^ mask
        member = (block // per_member) ^ (me % group)
        start = pl.multiple_of((block % per_member) * REQ_DEV, REQ_DEV)
        for m in range(batch):
            at = (p * batch + m) * REQ_DEV
            rows[at : at + REQ_DEV, :] = wide[member, m, pl.ds(start, REQ_DEV), :]
    half, width = keep.shape
    send[:, :width] = lax.dot_general(
        rows[half:, :].astype(jnp.bfloat16),
        weight[...],
        ROWS_LAST,
        preferred_element_type=jnp.float32,
    ).astype(jnp.bfloat16)
    keep[...] = lax.dot_general(
        rows[:half, :].astype(jnp.bfloat16),
        weight[...],
        ROWS_LAST,
        preferred_element_type=jnp.float32,
    )


def project(me, held, weight, masks):
    batch, members, width = held[0].shape
    group = len(held)
    count = len(masks) * batch * REQ_DEV
    whole = pl.BlockSpec(memory_space=pltpu.VMEM)
    return pl.pallas_call(
        functools.partial(project_kernel, group, masks),
        out_shape=[
            jax.ShapeDtypeStruct((count // 2, weight.shape[0]), jnp.float32),
            jax.ShapeDtypeStruct((count // 2, pl.cdiv(weight.shape[0], 128) * 128), jnp.bfloat16),
        ],
        in_specs=[pl.BlockSpec(memory_space=pltpu.SMEM)] + [whole] * (group + 1),
        out_specs=[whole] * 2,
        scratch_shapes=[
            pltpu.VMEM((group,) + held[0].shape, jnp.float32),
            pltpu.VMEM((count, width), jnp.float32),
        ],
        compiler_params=pltpu.CompilerParams(vmem_limit_bytes=LIMIT),
        name="project",
    )(me, *held, weight)


def expert_kernel(count, hidden, me_ref, *refs):
    pieces = refs[:count]
    w_gate, far_up, far_down = refs[count : count + 3]
    keep, send = refs[count + 3 : count + 5]
    rows, gates, active, w_up, w_down, up_done, down_done = refs[count + 5 :]
    units, width = w_gate.shape
    tiles = [slice(start, min(start + TILE, units)) for start in range(0, units, TILE)]
    up_copies, down_copies = [
        [
            pltpu.make_async_copy(
                far.at[pl.ds(some.start, some.stop - some.start)],
                near.at[pl.ds(some.start, some.stop - some.start)],
                done.at[index],
            )
            for index, some in enumerate(tiles)
        ]
        for far, near, done in ((far_up, w_up, up_done), (far_down, w_down, down_done))
    ]
    for copy in up_copies:
        copy.start()
    at = 0
    for piece in pieces:
        rows[at : at + piece.shape[0], :] = piece[...]
        at += piece.shape[0]
    for some in tiles:
        gates[:, some] = lax.dot_general(
            rows[:, :width], w_gate[some, :], ROWS_LAST, preferred_element_type=jnp.float32
        )
    for copy in down_copies:
        copy.start()
    for copy, some in zip(up_copies, tiles):
        copy.wait()
        gate = gates[:, some]
        up = lax.dot_general(
            rows[:, :width], w_up[some, :], ROWS_LAST, preferred_element_type=jnp.float32
        )
        active[:, some] = ((up + 1.0) * gate * jax.nn.sigmoid(1.702 * gate)).astype(jnp.bfloat16)
    base = width // 128 * 128
    tail = rows[:, base:].astype(jnp.float32)
    lane = lax.broadcasted_iota(jnp.int32, tail.shape, 1) - (width - base)
    deep = min(units, SPLIT * hidden)
    weights = []
    for start in range(0, units, deep):
        expert = (me_ref[0] * units + start) // (SPLIT * hidden)
        picked = (lane == expert) | (lane == expert + EXPERTS)
        weights.append(jnp.sum(jnp.where(picked, tail, 0.0), axis=1, keepdims=True))
    half = keep.shape[0]
    for copy in down_copies:
        copy.wait()
    for start in range(0, width, 2 * TILE):
        some = slice(start, min(start + 2 * TILE, width))
        out = 0.0
        for index, weight in enumerate(weights):
            part = slice(index * deep, (index + 1) * deep)
            out = out + weight * jnp.dot(
                active[:, part], w_down[part, some], preferred_element_type=jnp.float32
            )
        keep[:, some] = out[:half]
        send[:, some] = out[half:].astype(jnp.bfloat16)


def expert_sums(me, pieces, w_gate, w_up, w_down):
    hidden, width = w_down.shape[1:]
    units = w_down.shape[0] * hidden
    count = sum(piece.shape[0] for piece in pieces)
    whole = pl.BlockSpec(memory_space=pltpu.VMEM)
    tiles = pl.cdiv(units, TILE)
    return pl.pallas_call(
        functools.partial(expert_kernel, len(pieces), hidden),
        out_shape=[
            jax.ShapeDtypeStruct((count // 2, width), jnp.float32),
            jax.ShapeDtypeStruct((count // 2, pl.cdiv(width, 128) * 128), jnp.bfloat16),
        ],
        in_specs=[pl.BlockSpec(memory_space=pltpu.SMEM)] + [whole] * (len(pieces) + 1)
        + [pl.BlockSpec(memory_space=pl.ANY)] * 2,
        out_specs=[whole] * 2,
        scratch_shapes=[
            pltpu.VMEM((count, pieces[0].shape[1]), jnp.bfloat16),
            pltpu.VMEM((count, units), jnp.float32),
            pltpu.VMEM((count, units), jnp.bfloat16),
            pltpu.VMEM((units, width), jnp.bfloat16),
            pltpu.VMEM((units, width), jnp.bfloat16),
            pltpu.SemaphoreType.DMA((tiles,)),
            pltpu.SemaphoreType.DMA((tiles,)),
        ],
        compiler_params=pltpu.CompilerParams(vmem_limit_bytes=50 << 20),
        name="experts",
    )(
        me,
        *pieces,
        w_gate.swapaxes(1, 2).reshape(units, width),
        w_up.swapaxes(1, 2).reshape(units, width),
        w_down.reshape(units, width),
    )


def shards(queries, new_kv, cache, lengths, residual, o_proj, router, w_gate, w_up, w_down, routes):
    device_count = lax.axis_size("req")
    device_index = lax.axis_index("req")
    stages, masks = plan(device_count)
    group_size = max(1, device_count // KVH)
    width = residual.shape[2]
    block_rows = residual.shape[0] * residual.shape[1]
    me = device_index.astype(jnp.int32)[None]

    held = attention(lengths, me % group_size, queries, new_kv, cache, group_size)
    held = [held[0]] + [from_mask(held[r], r) for r in range(1, group_size)]
    summed = scatter_sum(*project(me, held, o_proj.T, masks), stages)

    attended = (residual.reshape(block_rows, width).astype(jnp.float32) + summed).astype(
        jnp.bfloat16
    )
    attended_wide = attended.astype(jnp.float32)
    normed = (
        attended_wide
        * lax.rsqrt(jnp.mean(attended_wide * attended_wide, axis=1, keepdims=True) + 1e-05)
    ).astype(jnp.bfloat16)
    logits = jnp.dot(normed, router, preferred_element_type=jnp.float32)
    chosen_one = routes.reshape(block_rows, -1)[:, :, None] == jnp.arange(EXPERTS)[None, None, :]
    chosen = jnp.sum(jnp.where(chosen_one, logits[:, None, :], 0.0), axis=2)
    gates = 1.0 / jnp.sum(jnp.exp(chosen[:, None, :] - chosen[:, :, None]), axis=2)
    dense = jnp.sum(jnp.where(chosen_one, gates[:, :, None], 0.0), axis=1)
    high = lax.reduce_precision(dense, 8, 7)
    payload = jnp.concatenate(
        [normed, high.astype(jnp.bfloat16), (dense - high).astype(jnp.bfloat16)], axis=1
    )

    pieces = gather_rows(payload, stages)
    mixture = scatter_sum(
        *expert_sums(me, pieces, w_gate, w_up, w_down), stages
    )
    layer = (attended_wide + mixture).astype(jnp.bfloat16)
    return attended.reshape(residual.shape), layer.reshape(residual.shape)


def solution(mesh):
    placed = (
        P(None, ("groups", "req"), None),
        P(None, ("groups", "req"), None),
        P(None, ("groups", "req"), None, None),
        P(None, "groups"),
        P(None, ("groups", "req"), None),
        P("req", None),
        P(),
        P("req", None, None),
        P("req", None, None),
        P("req", None, None),
        P(None, ("groups", "req"), None),
    )
    return jax.shard_map(
        shards,
        mesh=mesh,
        in_specs=placed,
        out_specs=(P(None, ("groups", "req"), None), P(None, ("groups", "req"), None)),
        check_vma=False,
    )
```

```python
import functools
import math

import jax
import jax.numpy as jnp
from jax import lax
from jax.experimental import pallas as pl
from jax.experimental.pallas import tpu as pltpu
from jax.sharding import PartitionSpec as P

HD = 64
KVH = 8
QPK = 8
EXPERTS = 16
SPLIT = 4
REQ_DEV = 8
TILE = 256
LIMIT = 16 << 20
ROWS_LAST = (((1,), (1,)), ((), ()))


def plan(device_count):
    bits = device_count.bit_length() - 1
    stages = [(0, 1)] if bits else []
    bit = 1
    while bit < bits:
        width = min(2, bits - bit)
        stages.append((bit, width))
        bit += width
    masks = [0]
    for bit, width in stages:
        masks = [mask | (r << bit) for mask in masks for r in range(1 << width)]
    return stages, masks


def from_mask(value, mask):
    pairs = [(source, source ^ mask) for source in range(lax.axis_size("req"))]
    return lax.ppermute(value, "req", pairs)


def scatter_sum(keep, send, stages):
    width = keep.shape[1]
    total = keep + from_mask(send, 1)[:, :width].astype(jnp.float32)
    for bit, bits in stages[1:]:
        size = total.shape[0] >> bits
        pieces = [total[r * size : (r + 1) * size] for r in range(1 << bits)]
        total = pieces[0]
        for r in range(1, 1 << bits):
            moved = from_mask(pieces[r].astype(jnp.bfloat16), r << bit)
            total = total + moved.astype(jnp.float32)
    return total


def gather_rows(rows, stages):
    pieces = [rows]
    for bit, bits in reversed(stages):
        if bit:
            held = jnp.concatenate(pieces, axis=0) if len(pieces) > 1 else pieces[0]
            pieces = [held] + [from_mask(held, r << bit) for r in range(1, 1 << bits)]
        else:
            pieces = pieces + [from_mask(piece, 1) for piece in pieces]
    return pieces


def attention_kernel(
    group, blocks, lengths, place, q_ref, kv_ref, cache_ref, *refs
):
    outs = refs[:group]
    query, scores, mixed = refs[group:]
    rows, window, pair = cache_ref.shape
    batch, block = pl.program_id(0), pl.program_id(1)
    low = lax.broadcasted_iota(jnp.int32, (rows, pair), 1) < HD
    for h in range(QPK):
        tile = q_ref[:, (h // 2) * pair : (h // 2 + 1) * pair].astype(jnp.float32)
        tile = tile * (1.0 / math.sqrt(HD))
        if h % 2:
            tile = pltpu.roll(tile, HD, 1)
        query[pl.ds(h, rows, stride=QPK), :] = jnp.where(low, tile, 0.0)
    fresh = kv_ref[...].astype(jnp.float32)
    fresh = jnp.broadcast_to(fresh[:, None, :], (rows, QPK, pair)).reshape(rows * QPK, pair)
    own = jnp.sum(query[...] * fresh, axis=1, keepdims=True)
    position = lax.broadcasted_iota(jnp.int32, (QPK, window), 1)
    first = place[0] * (rows * blocks) + block * rows
    for r in range(rows):
        part = slice(r * QPK, (r + 1) * QPK)
        found = lax.dot_general(
            query[part, :].astype(jnp.bfloat16),
            cache_ref[r],
            ROWS_LAST,
            preferred_element_type=jnp.float32,
        )
        scores[part, :] = jnp.where(position < lengths[batch, first + r], found, -jnp.inf)
    top = jnp.maximum(jnp.max(scores[...], axis=1, keepdims=True), own)
    weight = jnp.exp(scores[...] - top)
    weight_own = jnp.exp(own - top)
    total = jnp.sum(weight, axis=1, keepdims=True) + weight_own
    scores[...] = weight / total
    prob_own = (weight_own / total).astype(jnp.bfloat16).astype(jnp.float32)
    for r in range(rows):
        part = slice(r * QPK, (r + 1) * QPK)
        mixed[part, :] = jnp.dot(
            scores[part, :].astype(jnp.bfloat16), cache_ref[r], preferred_element_type=jnp.float32
        )
    mixed[...] = mixed[...] + prob_own * fresh
    heads = QPK // group
    for r in range(group):
        start = (place[0] ^ r) * heads
        for j in range(0, heads, 2):
            left = pltpu.roll(mixed[pl.ds(start + j, rows, stride=QPK), :], HD, 1)
            if heads == 1:
                outs[r][...] = left[:, :HD].astype(jnp.bfloat16)
            else:
                right = mixed[pl.ds(start + j + 1, rows, stride=QPK), :]
                outs[r][:, j * HD : (j + 2) * HD] = jnp.where(low, left, right).astype(
                    jnp.bfloat16
                )


def attention(lengths, place, queries, new_kv, cache, group, block=32):
    batch, rows, window, pair = cache.shape
    block = min(block, rows)
    width = QPK // group * HD
    return pl.pallas_call(
        functools.partial(attention_kernel, group, rows // block),
        out_shape=[jax.ShapeDtypeStruct((batch, rows, width), jnp.bfloat16)] * group,
        grid_spec=pltpu.PrefetchScalarGridSpec(
            num_scalar_prefetch=2,
            grid=(batch, rows // block),
            in_specs=[
                pl.BlockSpec((None, block, QPK * HD), lambda m, i, *_: (m, i, 0)),
                pl.BlockSpec((None, block, pair), lambda m, i, *_: (m, i, 0)),
                pl.BlockSpec((None, block, window, pair), lambda m, i, *_: (m, i, 0, 0)),
            ],
            out_specs=[pl.BlockSpec((None, block, width), lambda m, i, *_: (m, i, 0))] * group,
            scratch_shapes=[
                pltpu.VMEM((block * QPK, pair), jnp.float32),
                pltpu.VMEM((block * QPK, window), jnp.float32),
                pltpu.VMEM((block * QPK, pair), jnp.float32),
            ],
        ),
        compiler_params=pltpu.CompilerParams(vmem_limit_bytes=61 << 20),
        name="attention",
    )(lengths, place, queries, new_kv, cache)


def project_kernel(group, masks, me_ref, *refs):
    held = refs[:group]
    weight, keep, send, wide, rows = refs[group:]
    batch, members, width = held[0].shape
    for r in range(group):
        wide[r] = held[r][...].astype(jnp.float32)
    me = me_ref[0]
    per_member = members // REQ_DEV
    for p, mask in enumerate(masks):
        block = me ^ mask
        member = (block // per_member) ^ (me % group)
        start = pl.multiple_of((block % per_member) * REQ_DEV, REQ_DEV)
        for m in range(batch):
            at = (p * batch + m) * REQ_DEV
            rows[at : at + REQ_DEV, :] = wide[member, m, pl.ds(start, REQ_DEV), :]
    half, width = keep.shape
    send[:, :width] = lax.dot_general(
        rows[half:, :].astype(jnp.bfloat16),
        weight[...],
        ROWS_LAST,
        preferred_element_type=jnp.float32,
    ).astype(jnp.bfloat16)
    keep[...] = lax.dot_general(
        rows[:half, :].astype(jnp.bfloat16),
        weight[...],
        ROWS_LAST,
        preferred_element_type=jnp.float32,
    )


def project(me, held, weight, masks):
    batch, members, width = held[0].shape
    group = len(held)
    count = len(masks) * batch * REQ_DEV
    whole = pl.BlockSpec(memory_space=pltpu.VMEM)
    return pl.pallas_call(
        functools.partial(project_kernel, group, masks),
        out_shape=[
            jax.ShapeDtypeStruct((count // 2, weight.shape[0]), jnp.float32),
            jax.ShapeDtypeStruct((count // 2, pl.cdiv(weight.shape[0], 128) * 128), jnp.bfloat16),
        ],
        in_specs=[pl.BlockSpec(memory_space=pltpu.SMEM)] + [whole] * (group + 1),
        out_specs=[whole] * 2,
        scratch_shapes=[
            pltpu.VMEM((group,) + held[0].shape, jnp.float32),
            pltpu.VMEM((count, width), jnp.float32),
        ],
        compiler_params=pltpu.CompilerParams(vmem_limit_bytes=LIMIT),
        cost_estimate=pl.CostEstimate(flops=60000000000, bytes_accessed=150000000, transcendentals=0),
        name="project",
    )(me, *held, weight)


def expert_kernel(count, hidden, me_ref, *refs):
    pieces = refs[:count]
    w_gate, w_up, w_down = refs[count : count + 3]
    keep, send = refs[count + 3 : count + 5]
    rows, active = refs[count + 5 :]
    units, width = w_gate.shape
    at = 0
    for piece in pieces:
        rows[at : at + piece.shape[0], :] = piece[...]
        at += piece.shape[0]
    for start in range(0, units, TILE):
        some = slice(start, min(start + TILE, units))
        gate = lax.dot_general(
            rows[:, :width], w_gate[some, :], ROWS_LAST, preferred_element_type=jnp.float32
        )
        up = lax.dot_general(
            rows[:, :width], w_up[some, :], ROWS_LAST, preferred_element_type=jnp.float32
        )
        active[:, some] = ((up + 1.0) * gate * jax.nn.sigmoid(1.702 * gate)).astype(jnp.bfloat16)
    base = width // 128 * 128
    tail = rows[:, base:].astype(jnp.float32)
    lane = lax.broadcasted_iota(jnp.int32, tail.shape, 1) - (width - base)
    deep = min(units, SPLIT * hidden)
    weights = []
    for start in range(0, units, deep):
        expert = (me_ref[0] * units + start) // (SPLIT * hidden)
        picked = (lane == expert) | (lane == expert + EXPERTS)
        weights.append(jnp.sum(jnp.where(picked, tail, 0.0), axis=1, keepdims=True))
    half = keep.shape[0]
    for start in range(0, width, 2 * TILE):
        some = slice(start, min(start + 2 * TILE, width))
        out = 0.0
        for index, weight in enumerate(weights):
            part = slice(index * deep, (index + 1) * deep)
            out = out + weight * jnp.dot(
                active[:, part], w_down[part, some], preferred_element_type=jnp.float32
            )
        keep[:, some] = out[:half]
        send[:, some] = out[half:].astype(jnp.bfloat16)


def expert_sums(me, pieces, w_gate, w_up, w_down):
    hidden, width = w_down.shape[1:]
    units = w_down.shape[0] * hidden
    count = sum(piece.shape[0] for piece in pieces)
    whole = pl.BlockSpec(memory_space=pltpu.VMEM)
    return pl.pallas_call(
        functools.partial(expert_kernel, len(pieces), hidden),
        out_shape=[
            jax.ShapeDtypeStruct((count // 2, width), jnp.float32),
            jax.ShapeDtypeStruct((count // 2, pl.cdiv(width, 128) * 128), jnp.bfloat16),
        ],
        in_specs=[pl.BlockSpec(memory_space=pltpu.SMEM)] + [whole] * (len(pieces) + 3),
        out_specs=[whole] * 2,
        scratch_shapes=[
            pltpu.VMEM((count, pieces[0].shape[1]), jnp.bfloat16),
            pltpu.VMEM((count, units), jnp.bfloat16),
        ],
        compiler_params=pltpu.CompilerParams(vmem_limit_bytes=LIMIT),
        name="experts",
    )(
        me,
        *pieces,
        w_gate.swapaxes(1, 2).reshape(units, width),
        w_up.swapaxes(1, 2).reshape(units, width),
        w_down.reshape(units, width),
    )


def shards(queries, new_kv, cache, lengths, residual, o_proj, router, w_gate, w_up, w_down, routes):
    device_count = lax.axis_size("req")
    device_index = lax.axis_index("req")
    stages, masks = plan(device_count)
    group_size = max(1, device_count // KVH)
    width = residual.shape[2]
    block_rows = residual.shape[0] * residual.shape[1]
    me = device_index.astype(jnp.int32)[None]

    held = attention(lengths, me % group_size, queries, new_kv, cache, group_size)
    held = [held[0]] + [from_mask(held[r], r) for r in range(1, group_size)]
    summed = scatter_sum(*project(me, held, o_proj.T, masks), stages)

    attended = (residual.reshape(block_rows, width).astype(jnp.float32) + summed).astype(
        jnp.bfloat16
    )
    attended_wide = attended.astype(jnp.float32)
    normed = (
        attended_wide
        * lax.rsqrt(jnp.mean(attended_wide * attended_wide, axis=1, keepdims=True) + 1e-05)
    ).astype(jnp.bfloat16)
    logits = jnp.dot(normed, router, preferred_element_type=jnp.float32)
    chosen_one = routes.reshape(block_rows, -1)[:, :, None] == jnp.arange(EXPERTS)[None, None, :]
    chosen = jnp.sum(jnp.where(chosen_one, logits[:, None, :], 0.0), axis=2)
    gates = 1.0 / jnp.sum(jnp.exp(chosen[:, None, :] - chosen[:, :, None]), axis=2)
    dense = jnp.sum(jnp.where(chosen_one, gates[:, :, None], 0.0), axis=1)
    high = lax.reduce_precision(dense, 8, 7)
    payload = jnp.concatenate(
        [normed, high.astype(jnp.bfloat16), (dense - high).astype(jnp.bfloat16)], axis=1
    )

    pieces = gather_rows(payload, stages)
    mixture = scatter_sum(
        *expert_sums(me, pieces, w_gate, w_up, w_down), stages
    )
    layer = (attended_wide + mixture).astype(jnp.bfloat16)
    return attended.reshape(residual.shape), layer.reshape(residual.shape)


def solution(mesh):
    placed = (
        P(None, ("groups", "req"), None),
        P(None, ("groups", "req"), None),
        P(None, ("groups", "req"), None, None),
        P(None, "groups"),
        P(None, ("groups", "req"), None),
        P("req", None),
        P(),
        P("req", None, None),
        P("req", None, None),
        P("req", None, None),
        P(None, ("groups", "req"), None),
    )
    return jax.shard_map(
        shards,
        mesh=mesh,
        in_specs=placed,
        out_specs=(P(None, ("groups", "req"), None), P(None, ("groups", "req"), None)),
        check_vma=False,
    )
```

```python
import functools
import math

import jax
import jax.numpy as jnp
from jax import lax
from jax.experimental import pallas as pl
from jax.experimental.pallas import tpu as pltpu
from jax.sharding import PartitionSpec as P

HD = 64
KVH = 8
QPK = 8
EXPERTS = 16
SPLIT = 4
REQ_DEV = 8
TILE = 256
LANES = 128
LIMIT = 16 << 20
ROWS_LAST = (((1,), (1,)), ((), ()))


def plan(device_count):
    bits = device_count.bit_length() - 1
    stages, bit = [(0, 1)], 1
    while bit < bits - 1:
        width = min(2, bits - 1 - bit)
        stages.append((bit, width))
        bit += width
    stages.append((bits - 1, 1))
    masks = [0]
    for bit, width in stages:
        masks = [mask | (r << bit) for mask in masks for r in range(1 << width)]
    return stages, masks


def from_mask(value, mask):
    pairs = [(source, source ^ mask) for source in range(lax.axis_size("req"))]
    return lax.ppermute(value, "req", pairs)


def padded(width):
    return pl.cdiv(width, LANES) * LANES


def whole_call(kernel, name, outs, inputs, scratch=(), scalars=(), **options):
    return pl.pallas_call(
        kernel,
        out_shape=outs,
        in_specs=[pl.BlockSpec(memory_space=pltpu.SMEM)] * len(scalars)
        + [pl.BlockSpec(memory_space=pltpu.VMEM)] * len(inputs),
        out_specs=[pl.BlockSpec(memory_space=pltpu.VMEM)] * len(outs),
        scratch_shapes=list(scratch),
        compiler_params=pltpu.CompilerParams(vmem_limit_bytes=LIMIT),
        name=name,
        **options,
    )(*scalars, *inputs)


def split_kernel(count, *refs):
    total = refs[0][...]
    width = total.shape[1]
    for ref in refs[1:count]:
        total = total + ref[:, :width].astype(jnp.float32)
    outs = refs[count:]
    size = outs[0].shape[0]
    for r, out in enumerate(outs):
        out[...] = total[r * size : (r + 1) * size].astype(out.dtype)


def add_split(total, received, pieces):
    shape = (total.shape[0] // pieces, total.shape[1])
    return whole_call(
        functools.partial(split_kernel, 1 + len(received)),
        "add_split",
        [
            jax.ShapeDtypeStruct(shape, jnp.bfloat16 if r else jnp.float32)
            for r in range(pieces)
        ],
        [total, *received],
    )


def scatter_sum(keep, send, stages):
    pieces = [keep, send]
    for index, (bit, bits) in enumerate(stages[:-1]):
        received = [from_mask(pieces[r], r << bit) for r in range(1, 1 << bits)]
        if index + 2 < len(stages):
            pieces = add_split(pieces[0], received, 1 << stages[index + 1][1])
    return pieces[0], received


def gather_rows(pieces, stages):
    for bit, bits in reversed(stages):
        if bit:
            held = jnp.concatenate(pieces, axis=0) if len(pieces) > 1 else pieces[0]
            pieces = [held] + [from_mask(held, r << bit) for r in range(1, 1 << bits)]
        else:
            pieces = pieces + [from_mask(piece, 1) for piece in pieces]
    return pieces


def share_kernel(count, routes, *refs):
    received, residual = refs[:count], refs[count]
    total, message = refs[count + 1 :]
    rows, width = residual.shape
    value = received[0][...]
    for ref in received[1:]:
        value = value + ref[:, :width].astype(jnp.float32)
    total[:rows, :width] = value[:rows] + residual[...].astype(jnp.float32)
    total[rows:, :width] = value[rows:]
    message[:, :width] = total[:, :width].astype(jnp.bfloat16)
    base = width // LANES * LANES
    used = width - base
    lane = lax.broadcasted_iota(jnp.int32, (rows, LANES), 1)
    row = lax.broadcasted_iota(jnp.int32, (rows, LANES), 0)
    named = lane < 0
    batch, top, each = routes.shape
    for m in range(batch):
        for i in range(each):
            for t in range(top):
                named |= (row == m * each + i) & (lane == used + routes[m, t, i])
    end = jnp.where(lane < used, total[:rows, base:], jnp.where(named, 1.0, 0.0))
    message[:rows, base:] = end.astype(jnp.bfloat16)
    end = jnp.where(lane < used, total[rows:, base:], 0.0)
    message[rows:, base:] = end.astype(jnp.bfloat16)


def norm_kernel(total, mine, theirs, router, attended, payload):
    rows, width = attended.shape
    base = width // LANES * LANES
    used = width - base
    lane = lax.broadcasted_iota(jnp.int32, (rows, LANES), 1)
    place = lax.broadcasted_iota(jnp.int32, (EXPERTS, LANES), 1) - used
    place -= lax.broadcasted_iota(jnp.int32, (EXPERTS, LANES), 0)
    first = jnp.where(place == 0, 1.0, 0.0).astype(jnp.bfloat16)
    second = jnp.where(place == EXPERTS, 1.0, 0.0).astype(jnp.bfloat16)
    for half, source in enumerate((mine, theirs)):
        own = slice(half * rows, (half + 1) * rows)
        other = slice((1 - half) * rows, (2 - half) * rows)
        value = total[own, :width] + theirs[other, :width].astype(jnp.float32)
        value = value.astype(jnp.bfloat16)
        if half == 0:
            attended[...] = value
        value = value.astype(jnp.float32)
        mean = jnp.sum(value * value, axis=1, keepdims=True) * (1.0 / width)
        normed = (value * lax.rsqrt(mean + 1e-05)).astype(jnp.bfloat16)
        payload[own, :width] = normed
        logits = lax.dot_general(
            normed, router[...], ROWS_LAST, preferred_element_type=jnp.float32
        )
        named = lax.dot_general(
            source[:rows, base:], first, ROWS_LAST, preferred_element_type=jnp.float32
        )
        named = named > 0.5
        top = jnp.max(jnp.where(named, logits, -jnp.inf), axis=1, keepdims=True)
        weight = jnp.where(named, jnp.exp(jnp.where(named, logits - top, 0.0)), 0.0)
        gate = weight / jnp.sum(weight, axis=1, keepdims=True)
        high = gate.astype(jnp.bfloat16)
        low = (gate - high.astype(jnp.float32)).astype(jnp.bfloat16)
        end = jnp.dot(high, first, preferred_element_type=jnp.float32)
        end = end + jnp.dot(low, second, preferred_element_type=jnp.float32)
        kept = payload[own, base:].astype(jnp.float32)
        payload[own, base:] = jnp.where(lane < used, kept, end).astype(jnp.bfloat16)


def attend(total, received, residual, routes, router, stages):
    rows, width = residual.shape
    wide = padded(width)
    total, message = whole_call(
        functools.partial(share_kernel, 1 + len(received)),
        "share",
        [
            jax.ShapeDtypeStruct((2 * rows, wide), jnp.float32),
            jax.ShapeDtypeStruct((2 * rows, wide), jnp.bfloat16),
        ],
        [total, *received, residual],
        scalars=[routes],
    )
    theirs = from_mask(message, 1 << stages[-1][0])
    return whole_call(
        norm_kernel,
        "norm",
        [
            jax.ShapeDtypeStruct((rows, width), jnp.bfloat16),
            jax.ShapeDtypeStruct((2 * rows, wide), jnp.bfloat16),
        ],
        [total, message, theirs, router],
    )


def finish_kernel(total, received, attended, layer):
    value = total[...] + received[...].astype(jnp.float32)
    layer[...] = (attended[...].astype(jnp.float32) + value).astype(jnp.bfloat16)


def attention_kernel(
    group, blocks, lengths, place, q_ref, kv_ref, cache_ref, *refs
):
    outs = refs[:group]
    query, scores, mixed = refs[group:]
    rows, window, pair = cache_ref.shape
    batch, block = pl.program_id(0), pl.program_id(1)
    low = lax.broadcasted_iota(jnp.int32, (rows, pair), 1) < HD
    for h in range(QPK):
        tile = q_ref[:, (h // 2) * pair : (h // 2 + 1) * pair].astype(jnp.float32)
        tile = tile * (1.0 / math.sqrt(HD))
        if h % 2:
            tile = pltpu.roll(tile, HD, 1)
        query[pl.ds(h, rows, stride=QPK), :] = jnp.where(low, tile, 0.0)
    fresh = kv_ref[...].astype(jnp.float32)
    fresh = jnp.broadcast_to(fresh[:, None, :], (rows, QPK, pair)).reshape(rows * QPK, pair)
    own = jnp.sum(query[...] * fresh, axis=1, keepdims=True)
    position = lax.broadcasted_iota(jnp.int32, (QPK, window), 1)
    first = place[0] * (rows * blocks) + block * rows
    for r in range(rows):
        part = slice(r * QPK, (r + 1) * QPK)
        found = lax.dot_general(
            query[part, :].astype(jnp.bfloat16),
            cache_ref[r],
            ROWS_LAST,
            preferred_element_type=jnp.float32,
        )
        scores[part, :] = jnp.where(position < lengths[batch, first + r], found, -jnp.inf)
    top = jnp.maximum(jnp.max(scores[...], axis=1, keepdims=True), own)
    weight = jnp.exp(scores[...] - top)
    weight_own = jnp.exp(own - top)
    total = jnp.sum(weight, axis=1, keepdims=True) + weight_own
    scores[...] = weight / total
    prob_own = (weight_own / total).astype(jnp.bfloat16).astype(jnp.float32)
    for r in range(rows):
        part = slice(r * QPK, (r + 1) * QPK)
        mixed[part, :] = jnp.dot(
            scores[part, :].astype(jnp.bfloat16), cache_ref[r], preferred_element_type=jnp.float32
        )
    mixed[...] = mixed[...] + prob_own * fresh
    heads = QPK // group
    for r in range(group):
        start = (place[0] ^ r) * heads
        for j in range(0, heads, 2):
            left = pltpu.roll(mixed[pl.ds(start + j, rows, stride=QPK), :], HD, 1)
            if heads == 1:
                outs[r][...] = left[:, :HD].astype(jnp.bfloat16)
            else:
                right = mixed[pl.ds(start + j + 1, rows, stride=QPK), :]
                outs[r][:, j * HD : (j + 2) * HD] = jnp.where(low, left, right).astype(
                    jnp.bfloat16
                )


def attention(lengths, place, queries, new_kv, cache, group, block=32):
    batch, rows, window, pair = cache.shape
    block = min(block, rows)
    width = QPK // group * HD
    return pl.pallas_call(
        functools.partial(attention_kernel, group, rows // block),
        out_shape=[jax.ShapeDtypeStruct((batch, rows, width), jnp.bfloat16)] * group,
        grid_spec=pltpu.PrefetchScalarGridSpec(
            num_scalar_prefetch=2,
            grid=(batch, rows // block),
            in_specs=[
                pl.BlockSpec((None, block, QPK * HD), lambda m, i, *_: (m, i, 0)),
                pl.BlockSpec((None, block, pair), lambda m, i, *_: (m, i, 0)),
                pl.BlockSpec((None, block, window, pair), lambda m, i, *_: (m, i, 0, 0)),
            ],
            out_specs=[pl.BlockSpec((None, block, width), lambda m, i, *_: (m, i, 0))] * group,
            scratch_shapes=[
                pltpu.VMEM((block * QPK, pair), jnp.float32),
                pltpu.VMEM((block * QPK, window), jnp.float32),
                pltpu.VMEM((block * QPK, pair), jnp.float32),
            ],
        ),
        compiler_params=pltpu.CompilerParams(vmem_limit_bytes=61 << 20),
        name="attention",
    )(lengths, place, queries, new_kv, cache)


def project_kernel(group, masks, me_ref, *refs):
    held = refs[:group]
    weight, keep, send, wide, rows = refs[group:]
    batch, members, width = held[0].shape
    for r in range(group):
        wide[r] = held[r][...].astype(jnp.float32)
    me = me_ref[0]
    per_member = members // REQ_DEV
    for p, mask in enumerate(masks):
        block = me ^ mask
        member = (block // per_member) ^ (me % group)
        start = pl.multiple_of((block % per_member) * REQ_DEV, REQ_DEV)
        for m in range(batch):
            at = (p * batch + m) * REQ_DEV
            rows[at : at + REQ_DEV, :] = wide[member, m, pl.ds(start, REQ_DEV), :]
    half, width = keep.shape
    send[:, :width] = lax.dot_general(
        rows[half:, :].astype(jnp.bfloat16),
        weight[...],
        ROWS_LAST,
        preferred_element_type=jnp.float32,
    ).astype(jnp.bfloat16)
    keep[...] = lax.dot_general(
        rows[:half, :].astype(jnp.bfloat16),
        weight[...],
        ROWS_LAST,
        preferred_element_type=jnp.float32,
    )


def project(me, held, weight, masks):
    batch, members, width = held[0].shape
    group = len(held)
    count = len(masks) * batch * REQ_DEV
    whole = pl.BlockSpec(memory_space=pltpu.VMEM)
    return pl.pallas_call(
        functools.partial(project_kernel, group, masks),
        out_shape=[
            jax.ShapeDtypeStruct((count // 2, weight.shape[0]), jnp.float32),
            jax.ShapeDtypeStruct((count // 2, padded(weight.shape[0])), jnp.bfloat16),
        ],
        in_specs=[pl.BlockSpec(memory_space=pltpu.SMEM)] + [whole] * (group + 1),
        out_specs=[whole] * 2,
        scratch_shapes=[
            pltpu.VMEM((group,) + held[0].shape, jnp.float32),
            pltpu.VMEM((count, width), jnp.float32),
        ],
        compiler_params=pltpu.CompilerParams(vmem_limit_bytes=LIMIT),
        cost_estimate=pl.CostEstimate(flops=60_000_000_000, bytes_accessed=150_000_000, transcendentals=0),
        name="project",
    )(me, *held, weight)


def expert_kernel(count, hidden, me_ref, *refs):
    pieces = refs[:count]
    w_gate, w_up, w_down = refs[count : count + 3]
    keep, send = refs[count + 3 : count + 5]
    rows, active = refs[count + 5 :]
    units, width = w_gate.shape
    at = 0
    for piece in pieces:
        rows[at : at + piece.shape[0], :] = piece[...]
        at += piece.shape[0]
    for start in range(0, units, TILE):
        some = slice(start, min(start + TILE, units))
        gate = lax.dot_general(
            rows[:, :width], w_gate[some, :], ROWS_LAST, preferred_element_type=jnp.float32
        )
        up = lax.dot_general(
            rows[:, :width], w_up[some, :], ROWS_LAST, preferred_element_type=jnp.float32
        )
        active[:, some] = ((up + 1.0) * gate * jax.nn.sigmoid(1.702 * gate)).astype(jnp.bfloat16)
    base = width // 128 * 128
    tail = rows[:, base:].astype(jnp.float32)
    lane = lax.broadcasted_iota(jnp.int32, tail.shape, 1) - (width - base)
    deep = min(units, SPLIT * hidden)
    weights = []
    for start in range(0, units, deep):
        expert = (me_ref[0] * units + start) // (SPLIT * hidden)
        picked = (lane == expert) | (lane == expert + EXPERTS)
        weights.append(jnp.sum(jnp.where(picked, tail, 0.0), axis=1, keepdims=True))
    half = keep.shape[0]
    for start in range(0, width, 2 * TILE):
        some = slice(start, min(start + 2 * TILE, width))
        out = 0.0
        for index, weight in enumerate(weights):
            part = slice(index * deep, (index + 1) * deep)
            out = out + weight * jnp.dot(
                active[:, part], w_down[part, some], preferred_element_type=jnp.float32
            )
        keep[:, some] = out[:half]
        send[:, some] = out[half:].astype(jnp.bfloat16)


def expert_sums(me, pieces, w_gate, w_up, w_down):
    hidden, width = w_down.shape[1:]
    units = w_down.shape[0] * hidden
    count = sum(piece.shape[0] for piece in pieces)
    whole = pl.BlockSpec(memory_space=pltpu.VMEM)
    return pl.pallas_call(
        functools.partial(expert_kernel, len(pieces), hidden),
        out_shape=[
            jax.ShapeDtypeStruct((count // 2, width), jnp.float32),
            jax.ShapeDtypeStruct((count // 2, padded(width)), jnp.bfloat16),
        ],
        in_specs=[pl.BlockSpec(memory_space=pltpu.SMEM)] + [whole] * (len(pieces) + 3),
        out_specs=[whole] * 2,
        scratch_shapes=[
            pltpu.VMEM((count, pieces[0].shape[1]), jnp.bfloat16),
            pltpu.VMEM((count, units), jnp.bfloat16),
        ],
        compiler_params=pltpu.CompilerParams(vmem_limit_bytes=LIMIT),
        name="experts",
    )(
        me,
        *pieces,
        w_gate.swapaxes(1, 2).reshape(units, width),
        w_up.swapaxes(1, 2).reshape(units, width),
        w_down.reshape(units, width),
    )


def shards(queries, new_kv, cache, lengths, residual, o_proj, router, w_gate, w_up, w_down, routes):
    device_count = lax.axis_size("req")
    device_index = lax.axis_index("req")
    stages, masks = plan(device_count)
    group_size = max(1, device_count // KVH)
    batch, each, width = residual.shape
    me = device_index.astype(jnp.int32)[None]

    held = attention(lengths, me % group_size, queries, new_kv, cache, group_size)
    held = [held[0]] + [from_mask(held[r], r) for r in range(1, group_size)]
    total, received = scatter_sum(*project(me, held, o_proj.T, masks), stages)
    attended, payload = attend(
        total,
        received,
        residual.reshape(batch * each, width),
        routes.swapaxes(1, 2),
        router.T,
        stages,
    )
    pieces = gather_rows([payload], stages[:-1])
    total, received = scatter_sum(*expert_sums(me, pieces, w_gate, w_up, w_down), stages)
    kept, sent = add_split(total, received, 2)
    (layer,) = whole_call(
        finish_kernel,
        "finish",
        [jax.ShapeDtypeStruct(attended.shape, jnp.bfloat16)],
        [kept, from_mask(sent, 1 << stages[-1][0]), attended],
    )
    return attended.reshape(residual.shape), layer.reshape(residual.shape)


def solution(mesh):
    placed = (
        P(None, ("groups", "req"), None),
        P(None, ("groups", "req"), None),
        P(None, ("groups", "req"), None, None),
        P(None, "groups"),
        P(None, ("groups", "req"), None),
        P("req", None),
        P(),
        P("req", None, None),
        P("req", None, None),
        P("req", None, None),
        P(None, ("groups", "req"), None),
    )
    return jax.shard_map(
        shards,
        mesh=mesh,
        in_specs=placed,
        out_specs=(P(None, ("groups", "req"), None), P(None, ("groups", "req"), None)),
        check_vma=False,
    )
```

```python
import functools
import math

import jax
import jax.numpy as jnp
from jax import lax
from jax.experimental import pallas as pl
from jax.experimental.pallas import tpu as pltpu
from jax.sharding import PartitionSpec as P

HD = 64
KVH = 8
QPK = 8
EXPERTS = 16
SPLIT = 4
REQ_DEV = 8
TILE = 256
LANES = 128
COPY_ROWS = 16
COPIES_AHEAD = 8
LIMIT = 16 << 20
AHEAD = pl.CostEstimate(flops=60_000_000_000, bytes_accessed=150_000_000, transcendentals=0)
ROWS_LAST = (((1,), (1,)), ((), ()))


def plan(device_count):
    bits = device_count.bit_length() - 1
    stages, bit = [(0, 1)], 1
    while bit < bits - 1:
        width = min(2, bits - 1 - bit)
        stages.append((bit, width))
        bit += width
    stages.append((bits - 1, 1))
    masks = [0]
    for bit, width in stages:
        masks = [mask | (r << bit) for mask in masks for r in range(1 << width)]
    return stages, masks


def from_mask(value, mask):
    pairs = [(source, source ^ mask) for source in range(lax.axis_size("req"))]
    return lax.ppermute(value, "req", pairs)


def padded(width):
    return pl.cdiv(width, LANES) * LANES


def whole_call(kernel, name, outs, inputs, scratch=(), scalars=(), **options):
    return pl.pallas_call(
        kernel,
        out_shape=outs,
        in_specs=[pl.BlockSpec(memory_space=pltpu.SMEM)] * len(scalars)
        + [pl.BlockSpec(memory_space=pltpu.VMEM)] * len(inputs),
        out_specs=[pl.BlockSpec(memory_space=pltpu.VMEM)] * len(outs),
        scratch_shapes=list(scratch),
        compiler_params=pltpu.CompilerParams(vmem_limit_bytes=LIMIT),
        name=name,
        **options,
    )(*scalars, *inputs)


def split_kernel(count, pieces, *refs):
    total = refs[0][...]
    width = total.shape[1]
    for ref in refs[1:count]:
        total = total + ref[:, :width].astype(jnp.float32)
    outs = refs[count:]
    size = outs[0].shape[0]
    for index, out in enumerate(outs):
        out[...] = total[index * size : (index + 1) * size].astype(out.dtype)


def add_split(total, received, pieces, chunks=1):
    shape = (total.shape[0] // (pieces * chunks), total.shape[1])
    types = [jnp.float32] + [jnp.bfloat16] * (pieces - 1)
    found = whole_call(
        functools.partial(split_kernel, 1 + len(received), pieces),
        "add_split",
        [jax.ShapeDtypeStruct(shape, dtype) for dtype in types] * chunks,
        [total, *received],
    )
    return [found[c * pieces : (c + 1) * pieces] for c in range(chunks)]


def scatter_sum(pieces, stages):
    for index, (bit, bits) in enumerate(stages):
        received = [from_mask(pieces[r], r << bit) for r in range(1, 1 << bits)]
        if index + 1 < len(stages):
            (pieces,) = add_split(pieces[0], received, 1 << stages[index + 1][1])
    return pieces[0], received


def gather_rows(pieces, stages):
    for bit, bits in reversed(stages):
        if bit:
            held = jnp.concatenate(pieces, axis=0) if len(pieces) > 1 else pieces[0]
            pieces = [held] + [from_mask(held, r << bit) for r in range(1, 1 << bits)]
        else:
            pieces = pieces + [from_mask(piece, 1) for piece in pieces]
    return pieces


def share_kernel(batch, count, routes, *refs):
    received, residual = refs[:count], refs[count]
    total, message = refs[count + 1 :]
    rows, width = residual.shape[1:]
    value = received[0][...]
    for ref in received[1:]:
        value = value + ref[:, :width].astype(jnp.float32)
    total[:rows, :width] = value[:rows] + residual[batch].astype(jnp.float32)
    total[rows:, :width] = value[rows:]
    message[:, :width] = total[:, :width].astype(jnp.bfloat16)
    base = width // LANES * LANES
    used = width - base
    lane = lax.broadcasted_iota(jnp.int32, (2 * rows, LANES), 1)
    row = lax.broadcasted_iota(jnp.int32, (2 * rows, LANES), 0)
    named = lane < 0
    for i in range(routes.shape[2]):
        for t in range(routes.shape[1]):
            named |= (row == i) & (lane == used + routes[batch, t, i])
    end = jnp.where(lane < used, total[:, base:], jnp.where(named, 1.0, 0.0))
    message[:, base:] = end.astype(jnp.bfloat16)


def norm_kernel(total, mine, theirs, router, attended, payload):
    rows, width = attended.shape
    base = width // LANES * LANES
    used = width - base
    lane = lax.broadcasted_iota(jnp.int32, (2 * rows, LANES), 1)
    place = lax.broadcasted_iota(jnp.int32, (EXPERTS, LANES), 1) - used
    place -= lax.broadcasted_iota(jnp.int32, (EXPERTS, LANES), 0)
    first = jnp.where(place == 0, 1.0, 0.0).astype(jnp.bfloat16)
    second = jnp.where(place == EXPERTS, 1.0, 0.0).astype(jnp.bfloat16)
    other = theirs[...].astype(jnp.float32)
    swapped = jnp.concatenate([other[rows:, :width], other[:rows, :width]], axis=0)
    value = total[:, :width] + swapped
    attended[...] = value[:rows].astype(jnp.bfloat16)
    value = value.astype(jnp.bfloat16).astype(jnp.float32)
    mean = jnp.sum(value * value, axis=1, keepdims=True) * (1.0 / width)
    normed = (value * lax.rsqrt(mean + 1e-05)).astype(jnp.bfloat16)
    payload[:, :width] = normed
    logits = lax.dot_general(normed, router[...], ROWS_LAST, preferred_element_type=jnp.float32)
    ends = jnp.concatenate(
        [mine[:, base:].astype(jnp.float32)[:rows], other[:rows, base:]], axis=0
    )
    named = lax.dot_general(
        ends.astype(jnp.bfloat16), first, ROWS_LAST, preferred_element_type=jnp.float32
    )
    named = named > 0.5
    top = jnp.max(jnp.where(named, logits, -jnp.inf), axis=1, keepdims=True)
    weight = jnp.where(named, jnp.exp(jnp.where(named, logits - top, 0.0)), 0.0)
    gate = weight / jnp.sum(weight, axis=1, keepdims=True)
    high = gate.astype(jnp.bfloat16)
    low = (gate - high.astype(jnp.float32)).astype(jnp.bfloat16)
    end = jnp.dot(high, first, preferred_element_type=jnp.float32)
    end = end + jnp.dot(low, second, preferred_element_type=jnp.float32)
    kept = payload[:, base:].astype(jnp.float32)
    payload[:, base:] = jnp.where(lane < used, kept, end).astype(jnp.bfloat16)


def attend(batch, total, received, residual, routes, router, stages):
    rows, width = residual.shape[1:]
    wide = padded(width)
    total, message = whole_call(
        functools.partial(share_kernel, batch, 1 + len(received)),
        "share",
        [
            jax.ShapeDtypeStruct((2 * rows, wide), jnp.float32),
            jax.ShapeDtypeStruct((2 * rows, wide), jnp.bfloat16),
        ],
        [total, *received, residual],
        scalars=[routes],
        cost_estimate=pl.CostEstimate(flops=60000000000, bytes_accessed=180000000, transcendentals=0),
    )
    theirs = from_mask(message, 1 << stages[-1][0])
    return whole_call(
        norm_kernel,
        "norm",
        [
            jax.ShapeDtypeStruct((rows, width), jnp.bfloat16),
            jax.ShapeDtypeStruct((2 * rows, wide), jnp.bfloat16),
        ],
        [total, message, theirs, router],
    )


def finish_kernel(batch, *refs):
    rows = refs[:batch]
    sums = refs[batch:-2]
    attended, layer = refs[-2:]
    each = rows[0].shape[0]
    begin = 0
    for total, received in zip(sums[::2], sums[1::2]):
        size = total.shape[1]
        some = slice(begin, begin + size)
        value = total[...] + received[:, :size].astype(jnp.float32)
        for m in range(batch):
            mixture = value[m * each : (m + 1) * each]
            layer[m, :, some] = (rows[m][:, some].astype(jnp.float32) + mixture).astype(
                jnp.bfloat16
            )
        begin += size
    for m in range(batch):
        attended[m] = rows[m][...]


def attention_kernel(group, block, lengths, place, far_q, far_kv, far, *refs):
    outs = refs[:group]
    q_ref, kv_ref, near, query, scores, mixed, done = refs[group:]
    small = [
        pltpu.make_async_copy(far_q, q_ref, done.at[0]),
        pltpu.make_async_copy(far_kv, kv_ref, done.at[1]),
    ]
    for copy in small:
        copy.start()
    batch, rows, window, pair = near.shape
    steps = [(m, i) for m in range(batch) for i in range(0, rows, block)]
    size = min(COPY_ROWS, block)
    copies = [
        pltpu.make_async_copy(
            far.at[m, pl.ds(i, size)], near.at[m, pl.ds(i, size)], done.at[index + 2]
        )
        for index, (m, i) in enumerate((m, i) for m in range(batch) for i in range(0, rows, size))
    ]
    started = finished = 0
    low = lax.broadcasted_iota(jnp.int32, (block, pair), 1) < HD
    position = lax.broadcasted_iota(jnp.int32, (QPK, window), 1)
    heads = QPK // group
    for m, i in steps:
        while started < min(finished + COPIES_AHEAD, len(copies)):
            copies[started].start()
            started += 1
        some = slice(i, i + block)
        if finished == 0:
            for copy in small:
                copy.wait()
        for h in range(QPK):
            tile = q_ref[m, some, (h // 2) * pair : (h // 2 + 1) * pair].astype(jnp.float32)
            tile = tile * (1.0 / math.sqrt(HD))
            if h % 2:
                tile = pltpu.roll(tile, HD, 1)
            query[pl.ds(h, block, stride=QPK), :] = jnp.where(low, tile, 0.0)
        fresh = kv_ref[m, some, :].astype(jnp.float32)
        fresh = jnp.broadcast_to(fresh[:, None, :], (block, QPK, pair))
        fresh = fresh.reshape(block * QPK, pair)
        own = jnp.sum(query[...] * fresh, axis=1, keepdims=True)
        first = place[0] * rows + i
        for _ in range(block // size):
            copies[finished].wait()
            finished += 1
            if started < len(copies):
                copies[started].start()
                started += 1
        for r in range(block):
            part = slice(r * QPK, (r + 1) * QPK)
            found = lax.dot_general(
                query[part, :].astype(jnp.bfloat16),
                near[m, i + r],
                ROWS_LAST,
                preferred_element_type=jnp.float32,
            )
            scores[part, :] = jnp.where(position < lengths[m, first + r], found, -jnp.inf)
        top = jnp.maximum(jnp.max(scores[...], axis=1, keepdims=True), own)
        weight = jnp.exp(scores[...] - top)
        weight_own = jnp.exp(own - top)
        total = jnp.sum(weight, axis=1, keepdims=True) + weight_own
        scores[...] = weight / total
        prob_own = (weight_own / total).astype(jnp.bfloat16).astype(jnp.float32)
        for r in range(block):
            part = slice(r * QPK, (r + 1) * QPK)
            mixed[part, :] = jnp.dot(
                scores[part, :].astype(jnp.bfloat16),
                near[m, i + r],
                preferred_element_type=jnp.float32,
            )
        mixed[...] = mixed[...] + prob_own * fresh
        for r in range(group):
            start = (place[0] ^ r) * heads
            for j in range(0, heads, 2):
                left = pltpu.roll(mixed[pl.ds(start + j, block, stride=QPK), :], HD, 1)
                if heads == 1:
                    outs[r][m, some, :] = left[:, :HD].astype(jnp.bfloat16)
                else:
                    right = mixed[pl.ds(start + j + 1, block, stride=QPK), :]
                    outs[r][m, some, j * HD : (j + 2) * HD] = jnp.where(low, left, right).astype(
                        jnp.bfloat16
                    )


def attention(lengths, place, queries, new_kv, cache, group, block=64):
    batch, rows, window, pair = cache.shape
    block = min(block, rows)
    width = QPK // group * HD
    small = pl.BlockSpec(memory_space=pltpu.SMEM)
    whole = pl.BlockSpec(memory_space=pltpu.VMEM)
    return pl.pallas_call(
        functools.partial(attention_kernel, group, block),
        out_shape=[pltpu.VMEM((batch, rows, width), jnp.bfloat16)] * group,
        in_specs=[small] * 2 + [pl.BlockSpec(memory_space=pl.ANY)] * 3,
        out_specs=[whole] * group,
        scratch_shapes=[
            pltpu.VMEM(queries.shape, jnp.bfloat16),
            pltpu.VMEM(new_kv.shape, jnp.bfloat16),
            pltpu.VMEM(cache.shape, jnp.bfloat16),
            pltpu.VMEM((block * QPK, pair), jnp.float32),
            pltpu.VMEM((block * QPK, window), jnp.float32),
            pltpu.VMEM((block * QPK, pair), jnp.float32),
            pltpu.SemaphoreType.DMA((2 + batch * rows // min(COPY_ROWS, block),)),
        ],
        compiler_params=pltpu.CompilerParams(vmem_limit_bytes=56 << 20),
        cost_estimate=pl.CostEstimate(
            flops=10000000000, bytes_accessed=30000000, transcendentals=0
        ),
        name="attention",
    )(lengths, place, queries, new_kv, cache)


def project_kernel(group, masks, me_ref, *refs):
    held = refs[:group]
    weight, outs, wide, rows = refs[group], refs[group + 1 : -2], *refs[-2:]
    batch, members, width = held[0].shape
    for r in range(group):
        wide[r] = held[r][...].astype(jnp.float32)
    me = me_ref[0]
    per_member = members // REQ_DEV
    for p, mask in enumerate(masks):
        block = me ^ mask
        member = (block // per_member) ^ (me % group)
        start = pl.multiple_of((block % per_member) * REQ_DEV, REQ_DEV)
        for m in range(batch):
            at = (m * len(masks) + p) * REQ_DEV
            rows[at : at + REQ_DEV, :] = wide[member, m, pl.ds(start, REQ_DEV), :]
    half, width = outs[0].shape
    found = lax.dot_general(
        rows[...].astype(jnp.bfloat16),
        weight[...],
        ROWS_LAST,
        preferred_element_type=jnp.float32,
    )
    for index, out in enumerate(outs):
        out[:, :width] = found[index * half : (index + 1) * half].astype(out.dtype)


def project(me, held, weight, masks):
    batch, members, width = held[0].shape
    group = len(held)
    half = len(masks) * REQ_DEV // 2
    found = whole_call(
        functools.partial(project_kernel, group, masks),
        "project",
        [
            jax.ShapeDtypeStruct((half, weight.shape[0]), jnp.float32),
            jax.ShapeDtypeStruct((half, padded(weight.shape[0])), jnp.bfloat16),
        ]
        * batch,
        [*held, weight],
        scratch=[
            pltpu.VMEM((group,) + held[0].shape, jnp.float32),
            pltpu.VMEM((2 * batch * half, width), jnp.float32),
        ],
        scalars=[me],
    )
    return [found[2 * m : 2 * m + 2] for m in range(batch)]


def expert_kernel(batch, count, hidden, me_ref, *refs):
    pieces = refs[:count]
    w_gate, w_up, w_down = refs[count : count + 3]
    keep, send, active, weights, rows = refs[count + 3 :]
    units, width = w_gate.shape
    at = 0
    for piece in pieces:
        rows[at : at + piece.shape[0], :] = piece[...]
        at += piece.shape[0]
    for start in range(0, units, TILE):
        some = slice(start, min(start + TILE, units))
        gate = lax.dot_general(
            rows[:, :width], w_gate[some, :], ROWS_LAST, preferred_element_type=jnp.float32
        )
        up = lax.dot_general(
            rows[:, :width], w_up[some, :], ROWS_LAST, preferred_element_type=jnp.float32
        )
        active[:, some] = ((up + 1.0) * gate * jax.nn.sigmoid(1.702 * gate)).astype(jnp.bfloat16)
    base = width // LANES * LANES
    tail = rows[:, base:].astype(jnp.float32)
    lane = lax.broadcasted_iota(jnp.int32, tail.shape, 1) - (width - base)
    deep = min(units, SPLIT * hidden)
    for index in range(units // deep):
        expert = (me_ref[0] * units + index * deep) // (SPLIT * hidden)
        picked = (lane == expert) | (lane == expert + EXPERTS)
        weight = jnp.sum(jnp.where(picked, tail, 0.0), axis=1, keepdims=True)
        weights[index] = jnp.broadcast_to(weight, weights.shape[1:])
    down_kernel(batch, hidden, 0, active, weights, w_down, keep, send)


def down_kernel(batch, hidden, begin, active, weights, w_down, keep, send):
    units = w_down.shape[0]
    deep = min(units, SPLIT * hidden)
    half, width = keep.shape
    for start in range(0, width, 2 * TILE):
        some = slice(start, min(start + 2 * TILE, width))
        out = 0.0
        for index in range(units // deep):
            part = slice(index * deep, (index + 1) * deep)
            out = out + weights[index, :, :1] * jnp.dot(
                active[:, part],
                w_down[part, begin + some.start : begin + some.stop],
                preferred_element_type=jnp.float32,
            )
        blocks = half // (batch * REQ_DEV)
        for side, ref in enumerate((keep, send)):
            ordered = []
            for p in range(side * blocks, (side + 1) * blocks):
                for m in range(batch):
                    at = (m * 2 * blocks + p) * REQ_DEV
                    ordered.append(out[at : at + REQ_DEV])
            ref[:, some] = jnp.concatenate(ordered, axis=0).astype(ref.dtype)


def expert_sums(me, batch, pieces, w_gate, w_up, w_down):
    hidden, width = w_down.shape[1:]
    units = w_down.shape[0] * hidden
    count = sum(piece.shape[0] for piece in pieces)
    parts = max(1, units // (SPLIT * hidden))
    first = padded(pl.cdiv(width, 2))

    def halves(columns):
        return [
            jax.ShapeDtypeStruct((count // 2, columns), jnp.float32),
            jax.ShapeDtypeStruct((count // 2, padded(columns)), jnp.bfloat16),
        ]

    down = w_down.reshape(units, width)
    keep, send, active, weights = whole_call(
        functools.partial(expert_kernel, batch, len(pieces), hidden),
        "experts",
        halves(first)
        + [
            jax.ShapeDtypeStruct((count, units), jnp.bfloat16),
            jax.ShapeDtypeStruct((parts, count, LANES), jnp.float32),
        ],
        [
            *pieces,
            w_gate.swapaxes(1, 2).reshape(units, width),
            w_up.swapaxes(1, 2).reshape(units, width),
            down,
        ],
        scratch=[pltpu.VMEM((count, pieces[0].shape[1]), jnp.bfloat16)],
        scalars=[me],
    )
    rest = whole_call(
        functools.partial(down_kernel, batch, hidden, first),
        "down",
        halves(width - first),
        [active, weights, down],
    )
    return [(keep, send), rest]


def shards(queries, new_kv, cache, lengths, residual, o_proj, router, w_gate, w_up, w_down, routes):
    device_count = lax.axis_size("req")
    device_index = lax.axis_index("req")
    stages, masks = plan(device_count)
    group_size = max(1, device_count // KVH)
    batch = residual.shape[0]
    me = device_index.astype(jnp.int32)[None]

    held = attention(lengths, me % group_size, queries, new_kv, cache, group_size)
    held = [held[0]] + [from_mask(held[r], r) for r in range(1, group_size)]
    halves = project(me, held, o_proj.T, masks)
    attended, pieces = [], []
    for m in range(batch):
        total, received = scatter_sum(halves[m], stages[:-1])
        rows, payload = attend(
            m, total, received, residual, routes.swapaxes(1, 2), router.T, stages
        )
        attended.append(rows)
        pieces += gather_rows([payload], stages[:-1])
    sums = []
    for halves in expert_sums(me, batch, pieces, w_gate, w_up, w_down):
        total, (received,) = scatter_sum(halves, stages)
        sums += [total, received]
    return whole_call(
        functools.partial(finish_kernel, batch),
        "finish",
        [jax.ShapeDtypeStruct(residual.shape, jnp.bfloat16)] * 2,
        [*attended, *sums],
    )


def solution(mesh):
    placed = (
        P(None, ("groups", "req"), None),
        P(None, ("groups", "req"), None),
        P(None, ("groups", "req"), None, None),
        P(None, "groups"),
        P(None, ("groups", "req"), None),
        P("req", None),
        P(),
        P("req", None, None),
        P("req", None, None),
        P("req", None, None),
        P(None, ("groups", "req"), None),
    )
    return jax.shard_map(
        shards,
        mesh=mesh,
        in_specs=placed,
        out_specs=(P(None, ("groups", "req"), None), P(None, ("groups", "req"), None)),
        check_vma=False,
    )
```

```python
import functools
import math

import jax
import jax.numpy as jnp
from jax import lax
from jax.experimental import pallas as pl
from jax.experimental.pallas import tpu as pltpu
from jax.sharding import PartitionSpec as P

HD = 64
KVH = 8
QPK = 8
EXPERTS = 16
SPLIT = 4
REQ_DEV = 8
TILE = 256
LANES = 128
COPY_ROWS = 16
COPIES_AHEAD = 8
LIMIT = 16 << 20
AHEAD = pl.CostEstimate(flops=60_000_000_000, bytes_accessed=150_000_000, transcendentals=0)
ROWS_LAST = (((1,), (1,)), ((), ()))


def plan(device_count):
    bits = device_count.bit_length() - 1
    stages, bit = [(0, 1)], 1
    while bit < bits - 1:
        width = min(2, bits - 1 - bit)
        stages.append((bit, width))
        bit += width
    stages.append((bits - 1, 1))
    masks = [0]
    for bit, width in stages:
        masks = [mask | (r << bit) for mask in masks for r in range(1 << width)]
    return stages, masks


def from_mask(value, mask):
    pairs = [(source, source ^ mask) for source in range(lax.axis_size("req"))]
    return lax.ppermute(value, "req", pairs)


def padded(width):
    return pl.cdiv(width, LANES) * LANES


def whole_call(kernel, name, outs, inputs, scratch=(), scalars=(), **options):
    return pl.pallas_call(
        kernel,
        out_shape=outs,
        in_specs=[pl.BlockSpec(memory_space=pltpu.SMEM)] * len(scalars)
        + [pl.BlockSpec(memory_space=pltpu.VMEM)] * len(inputs),
        out_specs=[pl.BlockSpec(memory_space=pltpu.VMEM)] * len(outs),
        scratch_shapes=list(scratch),
        compiler_params=pltpu.CompilerParams(vmem_limit_bytes=LIMIT),
        name=name,
        **options,
    )(*scalars, *inputs)


def split_kernel(count, pieces, *refs):
    total = refs[0][...]
    width = total.shape[1]
    for ref in refs[1:count]:
        total = total + ref[:, :width].astype(jnp.float32)
    outs = refs[count:]
    size = outs[0].shape[0]
    for index, out in enumerate(outs):
        out[...] = total[index * size : (index + 1) * size].astype(out.dtype)


def add_split(total, received, pieces, chunks=1):
    shape = (total.shape[0] // (pieces * chunks), total.shape[1])
    types = [jnp.float32] + [jnp.bfloat16] * (pieces - 1)
    found = whole_call(
        functools.partial(split_kernel, 1 + len(received), pieces),
        "add_split",
        [jax.ShapeDtypeStruct(shape, dtype) for dtype in types] * chunks,
        [total, *received],
    )
    return [found[c * pieces : (c + 1) * pieces] for c in range(chunks)]


def scatter_sum(pieces, stages):
    for index, (bit, bits) in enumerate(stages):
        received = [from_mask(pieces[r], r << bit) for r in range(1, 1 << bits)]
        if index + 1 < len(stages):
            (pieces,) = add_split(pieces[0], received, 1 << stages[index + 1][1])
    return pieces[0], received


def join_kernel(*refs):
    at = 0
    for ref in refs[:-1]:
        refs[-1][at : at + ref.shape[0], :] = ref[...]
        at += ref.shape[0]


def join(pieces):
    if len(pieces) == 1:
        return pieces[0]
    shape = (sum(piece.shape[0] for piece in pieces), pieces[0].shape[1])
    (joined,) = whole_call(
        join_kernel, "join", [jax.ShapeDtypeStruct(shape, pieces[0].dtype)], pieces
    )
    return joined


def gather_rows(rows, stages):
    pieces = [rows]
    for bit, bits in reversed(stages):
        held = join(pieces)
        received = [from_mask(held, r << bit) for r in range(1, 1 << bits)]
        pieces = [held, *received] if bit else [*pieces, *received]
    return pieces


def share_kernel(batch, count, routes, *refs):
    received, residual = refs[:count], refs[count]
    total, message = refs[count + 1 :]
    rows, width = residual.shape[1:]
    value = received[0][...]
    for ref in received[1:]:
        value = value + ref[:, :width].astype(jnp.float32)
    total[:rows, :width] = value[:rows] + residual[batch].astype(jnp.float32)
    total[rows:, :width] = value[rows:]
    message[:, :width] = total[:, :width].astype(jnp.bfloat16)
    base = width // LANES * LANES
    used = width - base
    lane = lax.broadcasted_iota(jnp.int32, (2 * rows, LANES), 1)
    row = lax.broadcasted_iota(jnp.int32, (2 * rows, LANES), 0)
    named = lane < 0
    for i in range(routes.shape[2]):
        for t in range(routes.shape[1]):
            named |= (row == i) & (lane == used + routes[batch, t, i])
    end = jnp.where(lane < used, total[:, base:], jnp.where(named, 1.0, 0.0))
    message[:, base:] = end.astype(jnp.bfloat16)


def norm_kernel(total, mine, theirs, router, attended, payload):
    rows, width = attended.shape
    base = width // LANES * LANES
    used = width - base
    lane = lax.broadcasted_iota(jnp.int32, (2 * rows, LANES), 1)
    place = lax.broadcasted_iota(jnp.int32, (EXPERTS, LANES), 1) - used
    place -= lax.broadcasted_iota(jnp.int32, (EXPERTS, LANES), 0)
    first = jnp.where(place == 0, 1.0, 0.0).astype(jnp.bfloat16)
    second = jnp.where(place == EXPERTS, 1.0, 0.0).astype(jnp.bfloat16)
    other = theirs[...].astype(jnp.float32)
    swapped = jnp.concatenate([other[rows:, :width], other[:rows, :width]], axis=0)
    value = total[:, :width] + swapped
    attended[...] = value[:rows].astype(jnp.bfloat16)
    value = value.astype(jnp.bfloat16).astype(jnp.float32)
    mean = jnp.sum(value * value, axis=1, keepdims=True) * (1.0 / width)
    normed = (value * lax.rsqrt(mean + 1e-05)).astype(jnp.bfloat16)
    payload[:, :width] = normed
    logits = lax.dot_general(normed, router[...], ROWS_LAST, preferred_element_type=jnp.float32)
    ends = jnp.concatenate(
        [mine[:, base:].astype(jnp.float32)[:rows], other[:rows, base:]], axis=0
    )
    named = lax.dot_general(
        ends.astype(jnp.bfloat16), first, ROWS_LAST, preferred_element_type=jnp.float32
    )
    named = named > 0.5
    top = jnp.max(jnp.where(named, logits, -jnp.inf), axis=1, keepdims=True)
    weight = jnp.where(named, jnp.exp(jnp.where(named, logits - top, 0.0)), 0.0)
    gate = weight / jnp.sum(weight, axis=1, keepdims=True)
    high = gate.astype(jnp.bfloat16)
    low = (gate - high.astype(jnp.float32)).astype(jnp.bfloat16)
    end = jnp.dot(high, first, preferred_element_type=jnp.float32)
    end = end + jnp.dot(low, second, preferred_element_type=jnp.float32)
    kept = payload[:, base:].astype(jnp.float32)
    payload[:, base:] = jnp.where(lane < used, kept, end).astype(jnp.bfloat16)


def attend(batch, total, received, residual, routes, router, stages):
    rows, width = residual.shape[1:]
    wide = padded(width)
    total, message = whole_call(
        functools.partial(share_kernel, batch, 1 + len(received)),
        "share",
        [
            jax.ShapeDtypeStruct((2 * rows, wide), jnp.float32),
            jax.ShapeDtypeStruct((2 * rows, wide), jnp.bfloat16),
        ],
        [total, *received, residual],
        scalars=[routes],
        cost_estimate=pl.CostEstimate(flops=60000000000, bytes_accessed=180000000, transcendentals=0),
    )
    theirs = from_mask(message, 1 << stages[-1][0])
    return whole_call(
        norm_kernel,
        "norm",
        [
            jax.ShapeDtypeStruct((rows, width), jnp.bfloat16),
            jax.ShapeDtypeStruct((2 * rows, wide), jnp.bfloat16),
        ],
        [total, message, theirs, router],
    )


def finish_kernel(batch, *refs):
    rows = refs[:batch]
    sums = refs[batch:-2]
    attended, layer = refs[-2:]
    each = rows[0].shape[0]
    begin = 0
    for total, received in zip(sums[::2], sums[1::2]):
        size = total.shape[1]
        some = slice(begin, begin + size)
        value = total[...] + received[:, :size].astype(jnp.float32)
        for m in range(batch):
            mixture = value[m * each : (m + 1) * each]
            layer[m, :, some] = (rows[m][:, some].astype(jnp.float32) + mixture).astype(
                jnp.bfloat16
            )
        begin += size
    for m in range(batch):
        attended[m] = rows[m][...]


def attention_kernel(group, block, lengths, place, far_q, far_kv, far, *refs):
    outs = refs[:group]
    q_ref, kv_ref, near, query, scores, mixed, done = refs[group:]
    small = [
        pltpu.make_async_copy(far_q, q_ref, done.at[0]),
        pltpu.make_async_copy(far_kv, kv_ref, done.at[1]),
    ]
    for copy in small:
        copy.start()
    batch, rows, window, pair = near.shape
    steps = [(m, i) for m in range(batch) for i in range(0, rows, block)]
    size = min(COPY_ROWS, block)
    copies = [
        pltpu.make_async_copy(
            far.at[m, pl.ds(i, size)], near.at[m, pl.ds(i, size)], done.at[index + 2]
        )
        for index, (m, i) in enumerate((m, i) for m in range(batch) for i in range(0, rows, size))
    ]
    started = finished = 0
    low = lax.broadcasted_iota(jnp.int32, (block, pair), 1) < HD
    position = lax.broadcasted_iota(jnp.int32, (QPK, window), 1)
    heads = QPK // group
    for m, i in steps:
        while started < min(finished + COPIES_AHEAD, len(copies)):
            copies[started].start()
            started += 1
        some = slice(i, i + block)
        if finished == 0:
            for copy in small:
                copy.wait()
        for h in range(QPK):
            tile = q_ref[m, some, (h // 2) * pair : (h // 2 + 1) * pair].astype(jnp.float32)
            tile = tile * (1.0 / math.sqrt(HD))
            if h % 2:
                tile = pltpu.roll(tile, HD, 1)
            query[pl.ds(h, block, stride=QPK), :] = jnp.where(low, tile, 0.0)
        fresh = kv_ref[m, some, :].astype(jnp.float32)
        fresh = jnp.broadcast_to(fresh[:, None, :], (block, QPK, pair))
        fresh = fresh.reshape(block * QPK, pair)
        own = jnp.sum(query[...] * fresh, axis=1, keepdims=True)
        first = place[0] * rows + i
        for _ in range(block // size):
            copies[finished].wait()
            finished += 1
            if started < len(copies):
                copies[started].start()
                started += 1
        for r in range(block):
            part = slice(r * QPK, (r + 1) * QPK)
            found = lax.dot_general(
                query[part, :].astype(jnp.bfloat16),
                near[m, i + r],
                ROWS_LAST,
                preferred_element_type=jnp.float32,
            )
            scores[part, :] = jnp.where(position < lengths[m, first + r], found, -jnp.inf)
        top = jnp.maximum(jnp.max(scores[...], axis=1, keepdims=True), own)
        weight = jnp.exp(scores[...] - top)
        weight_own = jnp.exp(own - top)
        total = jnp.sum(weight, axis=1, keepdims=True) + weight_own
        scores[...] = weight / total
        prob_own = (weight_own / total).astype(jnp.bfloat16).astype(jnp.float32)
        for r in range(block):
            part = slice(r * QPK, (r + 1) * QPK)
            mixed[part, :] = jnp.dot(
                scores[part, :].astype(jnp.bfloat16),
                near[m, i + r],
                preferred_element_type=jnp.float32,
            )
        mixed[...] = mixed[...] + prob_own * fresh
        for r in range(group):
            start = (place[0] ^ r) * heads
            for j in range(0, heads, 2):
                left = pltpu.roll(mixed[pl.ds(start + j, block, stride=QPK), :], HD, 1)
                if heads == 1:
                    outs[r][m, some, :] = left[:, :HD].astype(jnp.bfloat16)
                else:
                    right = mixed[pl.ds(start + j + 1, block, stride=QPK), :]
                    outs[r][m, some, j * HD : (j + 2) * HD] = jnp.where(low, left, right).astype(
                        jnp.bfloat16
                    )


def attention(lengths, place, queries, new_kv, cache, group, block=64):
    batch, rows, window, pair = cache.shape
    block = min(block, rows)
    width = QPK // group * HD
    small = pl.BlockSpec(memory_space=pltpu.SMEM)
    whole = pl.BlockSpec(memory_space=pltpu.VMEM)
    return pl.pallas_call(
        functools.partial(attention_kernel, group, block),
        out_shape=[pltpu.VMEM((batch, rows, width), jnp.bfloat16)] * group,
        in_specs=[small] * 2 + [pl.BlockSpec(memory_space=pl.ANY)] * 3,
        out_specs=[whole] * group,
        scratch_shapes=[
            pltpu.VMEM(queries.shape, jnp.bfloat16),
            pltpu.VMEM(new_kv.shape, jnp.bfloat16),
            pltpu.VMEM(cache.shape, jnp.bfloat16),
            pltpu.VMEM((block * QPK, pair), jnp.float32),
            pltpu.VMEM((block * QPK, window), jnp.float32),
            pltpu.VMEM((block * QPK, pair), jnp.float32),
            pltpu.SemaphoreType.DMA((2 + batch * rows // min(COPY_ROWS, block),)),
        ],
        compiler_params=pltpu.CompilerParams(vmem_limit_bytes=56 << 20),
        cost_estimate=pl.CostEstimate(
            flops=10000000000, bytes_accessed=30000000, transcendentals=0
        ),
        name="attention",
    )(lengths, place, queries, new_kv, cache)


def project_kernel(group, masks, me_ref, *refs):
    held = refs[:group]
    weight, outs, wide, rows = refs[group], refs[group + 1 : -2], *refs[-2:]
    batch, members, width = held[0].shape
    for r in range(group):
        wide[r] = held[r][...].astype(jnp.float32)
    me = me_ref[0]
    per_member = members // REQ_DEV
    for p, mask in enumerate(masks):
        block = me ^ mask
        member = (block // per_member) ^ (me % group)
        start = pl.multiple_of((block % per_member) * REQ_DEV, REQ_DEV)
        for m in range(batch):
            at = (m * len(masks) + p) * REQ_DEV
            rows[at : at + REQ_DEV, :] = wide[member, m, pl.ds(start, REQ_DEV), :]
    half, width = outs[0].shape
    found = lax.dot_general(
        rows[...].astype(jnp.bfloat16),
        weight[...],
        ROWS_LAST,
        preferred_element_type=jnp.float32,
    )
    for index, out in enumerate(outs):
        out[:, :width] = found[index * half : (index + 1) * half].astype(out.dtype)


def project(me, held, weight, masks):
    batch, members, width = held[0].shape
    group = len(held)
    half = len(masks) * REQ_DEV // 2
    found = whole_call(
        functools.partial(project_kernel, group, masks),
        "project",
        [
            jax.ShapeDtypeStruct((half, weight.shape[0]), jnp.float32),
            jax.ShapeDtypeStruct((half, padded(weight.shape[0])), jnp.bfloat16),
        ]
        * batch,
        [*held, weight],
        scratch=[
            pltpu.VMEM((group,) + held[0].shape, jnp.float32),
            pltpu.VMEM((2 * batch * half, width), jnp.float32),
        ],
        scalars=[me],
    )
    return [found[2 * m : 2 * m + 2] for m in range(batch)]


def expert_kernel(batch, count, hidden, me_ref, *refs):
    pieces = refs[:count]
    w_gate, w_up, w_down = refs[count : count + 3]
    keep, send, active, weights, rows = refs[count + 3 :]
    units, width = w_gate.shape
    at = 0
    for piece in pieces:
        rows[at : at + piece.shape[0], :] = piece[...]
        at += piece.shape[0]
    for start in range(0, units, TILE):
        some = slice(start, min(start + TILE, units))
        gate = lax.dot_general(
            rows[:, :width], w_gate[some, :], ROWS_LAST, preferred_element_type=jnp.float32
        )
        up = lax.dot_general(
            rows[:, :width], w_up[some, :], ROWS_LAST, preferred_element_type=jnp.float32
        )
        active[:, some] = ((up + 1.0) * gate * jax.nn.sigmoid(1.702 * gate)).astype(jnp.bfloat16)
    base = width // LANES * LANES
    tail = rows[:, base:].astype(jnp.float32)
    lane = lax.broadcasted_iota(jnp.int32, tail.shape, 1) - (width - base)
    deep = min(units, SPLIT * hidden)
    for index in range(units // deep):
        expert = (me_ref[0] * units + index * deep) // (SPLIT * hidden)
        picked = (lane == expert) | (lane == expert + EXPERTS)
        weight = jnp.sum(jnp.where(picked, tail, 0.0), axis=1, keepdims=True)
        weights[index] = jnp.broadcast_to(weight, weights.shape[1:])
    down_kernel(batch, hidden, 0, active, weights, w_down, keep, send)


def down_kernel(batch, hidden, begin, active, weights, w_down, keep, send):
    units = w_down.shape[0]
    deep = min(units, SPLIT * hidden)
    half, width = keep.shape
    for start in range(0, width, 2 * TILE):
        some = slice(start, min(start + 2 * TILE, width))
        out = 0.0
        for index in range(units // deep):
            part = slice(index * deep, (index + 1) * deep)
            out = out + weights[index, :, :1] * jnp.dot(
                active[:, part],
                w_down[part, begin + some.start : begin + some.stop],
                preferred_element_type=jnp.float32,
            )
        blocks = half // (batch * REQ_DEV)
        for side, ref in enumerate((keep, send)):
            ordered = []
            for p in range(side * blocks, (side + 1) * blocks):
                for m in range(batch):
                    at = (m * 2 * blocks + p) * REQ_DEV
                    ordered.append(out[at : at + REQ_DEV])
            ref[:, some] = jnp.concatenate(ordered, axis=0).astype(ref.dtype)


def expert_sums(me, batch, pieces, w_gate, w_up, w_down):
    hidden, width = w_down.shape[1:]
    units = w_down.shape[0] * hidden
    count = sum(piece.shape[0] for piece in pieces)
    parts = max(1, units // (SPLIT * hidden))
    first = padded(pl.cdiv(width * 10, 16))

    def halves(columns):
        return [
            jax.ShapeDtypeStruct((count // 2, columns), jnp.float32),
            jax.ShapeDtypeStruct((count // 2, padded(columns)), jnp.bfloat16),
        ]

    down = w_down.reshape(units, width)
    keep, send, active, weights = whole_call(
        functools.partial(expert_kernel, batch, len(pieces), hidden),
        "experts",
        halves(first)
        + [
            jax.ShapeDtypeStruct((count, units), jnp.bfloat16),
            jax.ShapeDtypeStruct((parts, count, LANES), jnp.float32),
        ],
        [
            *pieces,
            w_gate.swapaxes(1, 2).reshape(units, width),
            w_up.swapaxes(1, 2).reshape(units, width),
            down,
        ],
        scratch=[pltpu.VMEM((count, pieces[0].shape[1]), jnp.bfloat16)],
        scalars=[me],
    )
    rest = whole_call(
        functools.partial(down_kernel, batch, hidden, first),
        "down",
        halves(width - first),
        [active, weights, down],
    )
    return [(keep, send), rest]


def shards(queries, new_kv, cache, lengths, residual, o_proj, router, w_gate, w_up, w_down, routes):
    device_count = lax.axis_size("req")
    device_index = lax.axis_index("req")
    stages, masks = plan(device_count)
    group_size = max(1, device_count // KVH)
    batch = residual.shape[0]
    me = device_index.astype(jnp.int32)[None]

    held = attention(lengths, me % group_size, queries, new_kv, cache, group_size)
    held = [held[0]] + [from_mask(held[r], r) for r in range(1, group_size)]
    halves = project(me, held, o_proj.T, masks)
    attended, pieces = [], []
    for m in range(batch):
        total, received = scatter_sum(halves[m], stages[:-1])
        rows, payload = attend(
            m, total, received, residual, routes.swapaxes(1, 2), router.T, stages
        )
        attended.append(rows)
        pieces += gather_rows(payload, stages[:-1])
    sums = []
    for halves in expert_sums(me, batch, pieces, w_gate, w_up, w_down):
        total, (received,) = scatter_sum(halves, stages)
        sums += [total, received]
    return whole_call(
        functools.partial(finish_kernel, batch),
        "finish",
        [jax.ShapeDtypeStruct(residual.shape, jnp.bfloat16)] * 2,
        [*attended, *sums],
    )


def solution(mesh):
    placed = (
        P(None, ("groups", "req"), None),
        P(None, ("groups", "req"), None),
        P(None, ("groups", "req"), None, None),
        P(None, "groups"),
        P(None, ("groups", "req"), None),
        P("req", None),
        P(),
        P("req", None, None),
        P("req", None, None),
        P("req", None, None),
        P(None, ("groups", "req"), None),
    )
    return jax.shard_map(
        shards,
        mesh=mesh,
        in_specs=placed,
        out_specs=(P(None, ("groups", "req"), None), P(None, ("groups", "req"), None)),
        check_vma=False,
    )
```

```python
import functools
import math

import jax
import jax.numpy as jnp
from jax import lax
from jax.experimental import pallas as pl
from jax.experimental.pallas import tpu as pltpu
from jax.sharding import PartitionSpec as P

HD = 64
KVH = 8
QPK = 8
EXPERTS = 16
SPLIT = 4
REQ_DEV = 8
TILE = 256
LANES = 128
COPY_ROWS = 16
COPIES_AHEAD = 8
LIMIT = 16 << 20
AHEAD = pl.CostEstimate(flops=60_000_000_000, bytes_accessed=150_000_000, transcendentals=0)
ROWS_LAST = (((1,), (1,)), ((), ()))


def plan(device_count):
    bits = device_count.bit_length() - 1
    stages, bit = [(0, 1)], 1
    while bit < bits - 1:
        width = min(2, bits - 1 - bit)
        stages.append((bit, width))
        bit += width
    stages.append((bits - 1, 1))
    masks = [0]
    for bit, width in stages:
        masks = [mask | (r << bit) for mask in masks for r in range(1 << width)]
    return stages, masks


def from_mask(value, mask):
    pairs = [(source, source ^ mask) for source in range(lax.axis_size("req"))]
    return lax.ppermute(value, "req", pairs)


def padded(width):
    return pl.cdiv(width, LANES) * LANES


def whole_call(kernel, name, outs, inputs, scratch=(), scalars=(), **options):
    return pl.pallas_call(
        kernel,
        out_shape=outs,
        in_specs=[pl.BlockSpec(memory_space=pltpu.SMEM)] * len(scalars)
        + [pl.BlockSpec(memory_space=pltpu.VMEM)] * len(inputs),
        out_specs=[pl.BlockSpec(memory_space=pltpu.VMEM)] * len(outs),
        scratch_shapes=list(scratch),
        compiler_params=pltpu.CompilerParams(vmem_limit_bytes=LIMIT),
        name=name,
        **options,
    )(*scalars, *inputs)


def split_kernel(count, pieces, *refs):
    total = refs[0][...]
    width = total.shape[1]
    for ref in refs[1:count]:
        total = total + ref[:, :width].astype(jnp.float32)
    outs = refs[count:]
    size = outs[0].shape[0]
    for index, out in enumerate(outs):
        out[...] = total[index * size : (index + 1) * size].astype(out.dtype)


def add_split(total, received, pieces, chunks=1):
    shape = (total.shape[0] // (pieces * chunks), total.shape[1])
    types = [jnp.float32] + [jnp.bfloat16] * (pieces - 1)
    found = whole_call(
        functools.partial(split_kernel, 1 + len(received), pieces),
        "add_split",
        [jax.ShapeDtypeStruct(shape, dtype) for dtype in types] * chunks,
        [total, *received],
    )
    return [found[c * pieces : (c + 1) * pieces] for c in range(chunks)]


def scatter_sum(pieces, stages):
    for index, (bit, bits) in enumerate(stages):
        received = [from_mask(pieces[r], r << bit) for r in range(1, 1 << bits)]
        if index + 1 < len(stages):
            (pieces,) = add_split(pieces[0], received, 1 << stages[index + 1][1])
    return pieces[0], received


def join_kernel(*refs):
    at = 0
    for ref in refs[:-1]:
        refs[-1][at : at + ref.shape[0], :] = ref[...]
        at += ref.shape[0]


def join(pieces):
    if len(pieces) == 1:
        return pieces[0]
    shape = (sum(piece.shape[0] for piece in pieces), pieces[0].shape[1])
    (joined,) = whole_call(
        join_kernel, "join", [jax.ShapeDtypeStruct(shape, pieces[0].dtype)], pieces
    )
    return joined


def gather_rows(rows, stages):
    pieces = [rows]
    for bit, bits in reversed(stages):
        held = join(pieces)
        received = [from_mask(held, r << bit) for r in range(1, 1 << bits)]
        pieces = [held, *received] if bit else [*pieces, *received]
    return pieces


def share_kernel(batch, count, routes, *refs):
    received, residual = refs[:count], refs[count]
    total, message = refs[count + 1 :]
    rows, width = residual.shape[1:]
    value = received[0][...]
    for ref in received[1:]:
        value = value + ref[:, :width].astype(jnp.float32)
    total[:rows, :width] = value[:rows] + residual[batch].astype(jnp.float32)
    total[rows:, :width] = value[rows:]
    message[:, :width] = total[:, :width].astype(jnp.bfloat16)
    base = width // LANES * LANES
    used = width - base
    lane = lax.broadcasted_iota(jnp.int32, (2 * rows, LANES), 1)
    row = lax.broadcasted_iota(jnp.int32, (2 * rows, LANES), 0)
    named = lane < 0
    for i in range(routes.shape[2]):
        for t in range(routes.shape[1]):
            named |= (row == i) & (lane == used + routes[batch, t, i])
    end = jnp.where(lane < used, total[:, base:], jnp.where(named, 1.0, 0.0))
    message[:, base:] = end.astype(jnp.bfloat16)


def norm_kernel(total, mine, theirs, router, attended, payload):
    rows, width = attended.shape
    base = width // LANES * LANES
    used = width - base
    lane = lax.broadcasted_iota(jnp.int32, (2 * rows, LANES), 1)
    place = lax.broadcasted_iota(jnp.int32, (EXPERTS, LANES), 1) - used
    place -= lax.broadcasted_iota(jnp.int32, (EXPERTS, LANES), 0)
    first = jnp.where(place == 0, 1.0, 0.0).astype(jnp.bfloat16)
    second = jnp.where(place == EXPERTS, 1.0, 0.0).astype(jnp.bfloat16)
    other = theirs[...].astype(jnp.float32)
    swapped = jnp.concatenate([other[rows:, :width], other[:rows, :width]], axis=0)
    value = total[:, :width] + swapped
    attended[...] = value[:rows].astype(jnp.bfloat16)
    value = value.astype(jnp.bfloat16).astype(jnp.float32)
    mean = jnp.sum(value * value, axis=1, keepdims=True) * (1.0 / width)
    normed = (value * lax.rsqrt(mean + 1e-05)).astype(jnp.bfloat16)
    payload[:, :width] = normed
    logits = lax.dot_general(normed, router[...], ROWS_LAST, preferred_element_type=jnp.float32)
    ends = jnp.concatenate(
        [mine[:, base:].astype(jnp.float32)[:rows], other[:rows, base:]], axis=0
    )
    named = lax.dot_general(
        ends.astype(jnp.bfloat16), first, ROWS_LAST, preferred_element_type=jnp.float32
    )
    named = named > 0.5
    top = jnp.max(jnp.where(named, logits, -jnp.inf), axis=1, keepdims=True)
    weight = jnp.where(named, jnp.exp(jnp.where(named, logits - top, 0.0)), 0.0)
    gate = weight / jnp.sum(weight, axis=1, keepdims=True)
    high = gate.astype(jnp.bfloat16)
    low = (gate - high.astype(jnp.float32)).astype(jnp.bfloat16)
    end = jnp.dot(high, first, preferred_element_type=jnp.float32)
    end = end + jnp.dot(low, second, preferred_element_type=jnp.float32)
    kept = payload[:, base:].astype(jnp.float32)
    payload[:, base:] = jnp.where(lane < used, kept, end).astype(jnp.bfloat16)


def attend(batch, total, received, residual, routes, router, stages):
    rows, width = residual.shape[1:]
    wide = padded(width)
    total, message = whole_call(
        functools.partial(share_kernel, batch, 1 + len(received)),
        "share",
        [
            jax.ShapeDtypeStruct((2 * rows, wide), jnp.float32),
            jax.ShapeDtypeStruct((2 * rows, wide), jnp.bfloat16),
        ],
        [total, *received, residual],
        scalars=[routes],
        cost_estimate=pl.CostEstimate(flops=60000000000, bytes_accessed=180000000, transcendentals=0),
    )
    theirs = from_mask(message, 1 << stages[-1][0])
    return whole_call(
        norm_kernel,
        "norm",
        [
            jax.ShapeDtypeStruct((rows, width), jnp.bfloat16),
            jax.ShapeDtypeStruct((2 * rows, wide), jnp.bfloat16),
        ],
        [total, message, theirs, router],
    )


def finish_kernel(batch, *refs):
    rows = refs[:batch]
    sums = refs[batch:-2]
    attended, layer = refs[-2:]
    each = rows[0].shape[0]
    begin = 0
    for total, received in zip(sums[::2], sums[1::2]):
        size = total.shape[1]
        some = slice(begin, begin + size)
        value = total[...] + received[:, :size].astype(jnp.float32)
        for m in range(batch):
            mixture = value[m * each : (m + 1) * each]
            layer[m, :, some] = (rows[m][:, some].astype(jnp.float32) + mixture).astype(
                jnp.bfloat16
            )
        begin += size
    for m in range(batch):
        attended[m] = rows[m][...]


def attention_kernel(group, block, lengths, place, far_q, far_kv, far, *refs):
    outs = refs[:group]
    q_ref, kv_ref, near, query, scores, mixed, done = refs[group:]
    small = [
        pltpu.make_async_copy(far_q, q_ref, done.at[0]),
        pltpu.make_async_copy(far_kv, kv_ref, done.at[1]),
    ]
    for copy in small:
        copy.start()
    batch, rows, window, pair = near.shape
    steps = [(m, i) for m in range(batch) for i in range(0, rows, block)]
    size = min(COPY_ROWS, block)
    copies = [
        pltpu.make_async_copy(
            far.at[m, pl.ds(i, size)], near.at[m, pl.ds(i, size)], done.at[index + 2]
        )
        for index, (m, i) in enumerate((m, i) for m in range(batch) for i in range(0, rows, size))
    ]
    started = finished = 0
    low = lax.broadcasted_iota(jnp.int32, (block, pair), 1) < HD
    position = lax.broadcasted_iota(jnp.int32, (QPK, window), 1)
    upper = lax.broadcasted_iota(jnp.int32, (2 * QPK, window), 0) < QPK
    heads = QPK // group
    for m, i in steps:
        while started < min(finished + COPIES_AHEAD, len(copies)):
            copies[started].start()
            started += 1
        some = slice(i, i + block)
        if finished == 0:
            for copy in small:
                copy.wait()
        for h in range(QPK):
            tile = q_ref[m, some, (h // 2) * pair : (h // 2 + 1) * pair].astype(jnp.float32)
            tile = tile * (1.0 / math.sqrt(HD))
            if h % 2:
                tile = pltpu.roll(tile, HD, 1)
            query[pl.ds(h, block, stride=QPK), :] = jnp.where(low, tile, 0.0)
        fresh = kv_ref[m, some, :].astype(jnp.float32)
        fresh = jnp.broadcast_to(fresh[:, None, :], (block, QPK, pair))
        fresh = fresh.reshape(block * QPK, pair)
        own = jnp.sum(query[...] * fresh, axis=1, keepdims=True)
        first = place[0] * rows + i
        for _ in range(block // size):
            copies[finished].wait()
            finished += 1
            if started < len(copies):
                copies[started].start()
                started += 1
        for r in range(0, block, 2):
            part = slice(r * QPK, (r + 2) * QPK)
            found = lax.dot_general(
                query[part, :].astype(jnp.bfloat16),
                near[m, i + r : i + r + 2].reshape(2 * window, pair),
                ROWS_LAST,
                preferred_element_type=jnp.float32,
            )
            for k in (0, 1):
                own_part = found[k * QPK : (k + 1) * QPK, k * window : (k + 1) * window]
                scores[(r + k) * QPK : (r + k + 1) * QPK, :] = jnp.where(
                    position < lengths[m, first + r + k], own_part, -jnp.inf
                )
        top = jnp.maximum(jnp.max(scores[...], axis=1, keepdims=True), own)
        weight = jnp.exp(scores[...] - top)
        weight_own = jnp.exp(own - top)
        total = jnp.sum(weight, axis=1, keepdims=True) + weight_own
        scores[...] = weight / total
        prob_own = (weight_own / total).astype(jnp.bfloat16).astype(jnp.float32)
        for r in range(0, block, 2):
            part = slice(r * QPK, (r + 2) * QPK)
            prob = scores[part, :]
            prob = jnp.concatenate(
                [jnp.where(upper, prob, 0.0), jnp.where(upper, 0.0, prob)], axis=1
            )
            mixed[part, :] = jnp.dot(
                prob.astype(jnp.bfloat16),
                near[m, i + r : i + r + 2].reshape(2 * window, pair),
                preferred_element_type=jnp.float32,
            )
        mixed[...] = mixed[...] + prob_own * fresh
        for r in range(group):
            start = (place[0] ^ r) * heads
            for j in range(0, heads, 2):
                left = pltpu.roll(mixed[pl.ds(start + j, block, stride=QPK), :], HD, 1)
                if heads == 1:
                    outs[r][m, some, :] = left[:, :HD].astype(jnp.bfloat16)
                else:
                    right = mixed[pl.ds(start + j + 1, block, stride=QPK), :]
                    outs[r][m, some, j * HD : (j + 2) * HD] = jnp.where(low, left, right).astype(
                        jnp.bfloat16
                    )


def attention(lengths, place, queries, new_kv, cache, group, block=64):
    batch, rows, window, pair = cache.shape
    block = min(block, rows)
    width = QPK // group * HD
    small = pl.BlockSpec(memory_space=pltpu.SMEM)
    whole = pl.BlockSpec(memory_space=pltpu.VMEM)
    return pl.pallas_call(
        functools.partial(attention_kernel, group, block),
        out_shape=[pltpu.VMEM((batch, rows, width), jnp.bfloat16)] * group,
        in_specs=[small] * 2 + [pl.BlockSpec(memory_space=pl.ANY)] * 3,
        out_specs=[whole] * group,
        scratch_shapes=[
            pltpu.VMEM(queries.shape, jnp.bfloat16),
            pltpu.VMEM(new_kv.shape, jnp.bfloat16),
            pltpu.VMEM(cache.shape, jnp.bfloat16),
            pltpu.VMEM((block * QPK, pair), jnp.float32),
            pltpu.VMEM((block * QPK, window), jnp.float32),
            pltpu.VMEM((block * QPK, pair), jnp.float32),
            pltpu.SemaphoreType.DMA((2 + batch * rows // min(COPY_ROWS, block),)),
        ],
        compiler_params=pltpu.CompilerParams(vmem_limit_bytes=56 << 20),
        cost_estimate=pl.CostEstimate(
            flops=10000000000, bytes_accessed=30000000, transcendentals=0
        ),
        name="attention",
    )(lengths, place, queries, new_kv, cache)


def project_kernel(group, masks, me_ref, *refs):
    held = refs[:group]
    weight, outs, wide, rows = refs[group], refs[group + 1 : -2], *refs[-2:]
    batch, members, width = held[0].shape
    for r in range(group):
        wide[r] = held[r][...].astype(jnp.float32)
    me = me_ref[0]
    per_member = members // REQ_DEV
    for p, mask in enumerate(masks):
        block = me ^ mask
        member = (block // per_member) ^ (me % group)
        start = pl.multiple_of((block % per_member) * REQ_DEV, REQ_DEV)
        for m in range(batch):
            at = (m * len(masks) + p) * REQ_DEV
            rows[at : at + REQ_DEV, :] = wide[member, m, pl.ds(start, REQ_DEV), :]
    half, width = outs[0].shape
    found = lax.dot_general(
        rows[...].astype(jnp.bfloat16),
        weight[...],
        ROWS_LAST,
        preferred_element_type=jnp.float32,
    )
    for index, out in enumerate(outs):
        out[:, :width] = found[index * half : (index + 1) * half].astype(out.dtype)


def project(me, held, weight, masks):
    batch, members, width = held[0].shape
    group = len(held)
    half = len(masks) * REQ_DEV // 2
    found = whole_call(
        functools.partial(project_kernel, group, masks),
        "project",
        [
            jax.ShapeDtypeStruct((half, weight.shape[0]), jnp.float32),
            jax.ShapeDtypeStruct((half, padded(weight.shape[0])), jnp.bfloat16),
        ]
        * batch,
        [*held, weight],
        scratch=[
            pltpu.VMEM((group,) + held[0].shape, jnp.float32),
            pltpu.VMEM((2 * batch * half, width), jnp.float32),
        ],
        scalars=[me],
    )
    return [found[2 * m : 2 * m + 2] for m in range(batch)]


def expert_kernel(batch, count, hidden, me_ref, *refs):
    pieces = refs[:count]
    w_gate, w_up, w_down = refs[count : count + 3]
    keep, send, active, weights, rows = refs[count + 3 :]
    units, width = w_gate.shape
    at = 0
    for piece in pieces:
        rows[at : at + piece.shape[0], :] = piece[...]
        at += piece.shape[0]
    for start in range(0, units, TILE):
        some = slice(start, min(start + TILE, units))
        gate = lax.dot_general(
            rows[:, :width], w_gate[some, :], ROWS_LAST, preferred_element_type=jnp.float32
        )
        up = lax.dot_general(
            rows[:, :width], w_up[some, :], ROWS_LAST, preferred_element_type=jnp.float32
        )
        active[:, some] = ((up + 1.0) * gate * jax.nn.sigmoid(1.702 * gate)).astype(jnp.bfloat16)
    base = width // LANES * LANES
    tail = rows[:, base:].astype(jnp.float32)
    lane = lax.broadcasted_iota(jnp.int32, tail.shape, 1) - (width - base)
    deep = min(units, SPLIT * hidden)
    for index in range(units // deep):
        expert = (me_ref[0] * units + index * deep) // (SPLIT * hidden)
        picked = (lane == expert) | (lane == expert + EXPERTS)
        weight = jnp.sum(jnp.where(picked, tail, 0.0), axis=1, keepdims=True)
        weights[index] = jnp.broadcast_to(weight, weights.shape[1:])
    down_kernel(batch, hidden, 0, active, weights, w_down, keep, send)


def down_kernel(batch, hidden, begin, active, weights, w_down, keep, send):
    units = w_down.shape[0]
    deep = min(units, SPLIT * hidden)
    half, width = keep.shape
    for start in range(0, width, 2 * TILE):
        some = slice(start, min(start + 2 * TILE, width))
        out = 0.0
        for index in range(units // deep):
            part = slice(index * deep, (index + 1) * deep)
            out = out + weights[index, :, :1] * jnp.dot(
                active[:, part],
                w_down[part, begin + some.start : begin + some.stop],
                preferred_element_type=jnp.float32,
            )
        blocks = half // (batch * REQ_DEV)
        for side, ref in enumerate((keep, send)):
            ordered = []
            for p in range(side * blocks, (side + 1) * blocks):
                for m in range(batch):
                    at = (m * 2 * blocks + p) * REQ_DEV
                    ordered.append(out[at : at + REQ_DEV])
            ref[:, some] = jnp.concatenate(ordered, axis=0).astype(ref.dtype)


def expert_sums(me, batch, pieces, w_gate, w_up, w_down):
    hidden, width = w_down.shape[1:]
    units = w_down.shape[0] * hidden
    count = sum(piece.shape[0] for piece in pieces)
    parts = max(1, units // (SPLIT * hidden))
    first = padded(pl.cdiv(width * 10, 16))

    def halves(columns):
        return [
            jax.ShapeDtypeStruct((count // 2, columns), jnp.float32),
            jax.ShapeDtypeStruct((count // 2, padded(columns)), jnp.bfloat16),
        ]

    down = w_down.reshape(units, width)
    keep, send, active, weights = whole_call(
        functools.partial(expert_kernel, batch, len(pieces), hidden),
        "experts",
        halves(first)
        + [
            jax.ShapeDtypeStruct((count, units), jnp.bfloat16),
            jax.ShapeDtypeStruct((parts, count, LANES), jnp.float32),
        ],
        [
            *pieces,
            w_gate.swapaxes(1, 2).reshape(units, width),
            w_up.swapaxes(1, 2).reshape(units, width),
            down,
        ],
        scratch=[pltpu.VMEM((count, pieces[0].shape[1]), jnp.bfloat16)],
        scalars=[me],
    )
    rest = whole_call(
        functools.partial(down_kernel, batch, hidden, first),
        "down",
        halves(width - first),
        [active, weights, down],
    )
    return [(keep, send), rest]


def shards(queries, new_kv, cache, lengths, residual, o_proj, router, w_gate, w_up, w_down, routes):
    device_count = lax.axis_size("req")
    device_index = lax.axis_index("req")
    stages, masks = plan(device_count)
    group_size = max(1, device_count // KVH)
    batch = residual.shape[0]
    me = device_index.astype(jnp.int32)[None]

    held = attention(lengths, me % group_size, queries, new_kv, cache, group_size)
    held = [held[0]] + [from_mask(held[r], r) for r in range(1, group_size)]
    halves = project(me, held, o_proj.T, masks)
    attended, pieces = [], []
    for m in range(batch):
        total, received = scatter_sum(halves[m], stages[:-1])
        rows, payload = attend(
            m, total, received, residual, routes.swapaxes(1, 2), router.T, stages
        )
        attended.append(rows)
        pieces += gather_rows(payload, stages[:-1])
    sums = []
    for halves in expert_sums(me, batch, pieces, w_gate, w_up, w_down):
        total, (received,) = scatter_sum(halves, stages)
        sums += [total, received]
    return whole_call(
        functools.partial(finish_kernel, batch),
        "finish",
        [jax.ShapeDtypeStruct(residual.shape, jnp.bfloat16)] * 2,
        [*attended, *sums],
    )


def solution(mesh):
    placed = (
        P(None, ("groups", "req"), None),
        P(None, ("groups", "req"), None),
        P(None, ("groups", "req"), None, None),
        P(None, "groups"),
        P(None, ("groups", "req"), None),
        P("req", None),
        P(),
        P("req", None, None),
        P("req", None, None),
        P("req", None, None),
        P(None, ("groups", "req"), None),
    )
    return jax.shard_map(
        shards,
        mesh=mesh,
        in_specs=placed,
        out_specs=(P(None, ("groups", "req"), None), P(None, ("groups", "req"), None)),
        check_vma=False,
    )
```

```python
import functools
import math

import jax
import jax.numpy as jnp
from jax import lax
from jax.experimental import pallas as pl
from jax.experimental.pallas import tpu as pltpu
from jax.sharding import PartitionSpec as P

HD = 64
KVH = 8
QPK = 8
EXPERTS = 16
SPLIT = 4
REQ_DEV = 8
TILE = 256
LANES = 128
COPY_ROWS = 16
COPIES_AHEAD = 8
LIMIT = 16 << 20
AHEAD = pl.CostEstimate(flops=60_000_000_000, bytes_accessed=150_000_000, transcendentals=0)
ROWS_LAST = (((1,), (1,)), ((), ()))


def plan(device_count):
    bits = device_count.bit_length() - 1
    stages, bit = [(0, 1)], 1
    while bit < bits - 1:
        width = min(2, bits - 1 - bit)
        stages.append((bit, width))
        bit += width
    stages.append((bits - 1, 1))
    masks = [0]
    for bit, width in stages:
        masks = [mask | (r << bit) for mask in masks for r in range(1 << width)]
    return stages, masks


def from_mask(value, mask):
    pairs = [(source, source ^ mask) for source in range(lax.axis_size("req"))]
    return lax.ppermute(value, "req", pairs)


def padded(width):
    return pl.cdiv(width, LANES) * LANES


def whole_call(kernel, name, outs, inputs, scratch=(), scalars=(), **options):
    return pl.pallas_call(
        kernel,
        out_shape=outs,
        in_specs=[pl.BlockSpec(memory_space=pltpu.SMEM)] * len(scalars)
        + [pl.BlockSpec(memory_space=pltpu.VMEM)] * len(inputs),
        out_specs=[pl.BlockSpec(memory_space=pltpu.VMEM)] * len(outs),
        scratch_shapes=list(scratch),
        compiler_params=pltpu.CompilerParams(vmem_limit_bytes=LIMIT),
        name=name,
        **options,
    )(*scalars, *inputs)


def split_kernel(count, pieces, *refs):
    total = refs[0][...]
    width = total.shape[1]
    for ref in refs[1:count]:
        total = total + ref[:, :width].astype(jnp.float32)
    outs = refs[count:]
    size = outs[0].shape[0]
    for index, out in enumerate(outs):
        out[...] = total[index * size : (index + 1) * size].astype(out.dtype)


def add_split(total, received, pieces, chunks=1):
    shape = (total.shape[0] // (pieces * chunks), total.shape[1])
    types = [jnp.float32] + [jnp.bfloat16] * (pieces - 1)
    found = whole_call(
        functools.partial(split_kernel, 1 + len(received), pieces),
        "add_split",
        [jax.ShapeDtypeStruct(shape, dtype) for dtype in types] * chunks,
        [total, *received],
    )
    return [found[c * pieces : (c + 1) * pieces] for c in range(chunks)]


def scatter_sum(pieces, stages):
    for index, (bit, bits) in enumerate(stages):
        received = [from_mask(pieces[r], r << bit) for r in range(1, 1 << bits)]
        if index + 1 < len(stages):
            (pieces,) = add_split(pieces[0], received, 1 << stages[index + 1][1])
    return pieces[0], received


def join_kernel(*refs):
    at = 0
    for ref in refs[:-1]:
        refs[-1][at : at + ref.shape[0], :] = ref[...]
        at += ref.shape[0]


def join(pieces):
    if len(pieces) == 1:
        return pieces[0]
    shape = (sum(piece.shape[0] for piece in pieces), pieces[0].shape[1])
    (joined,) = whole_call(
        join_kernel, "join", [jax.ShapeDtypeStruct(shape, pieces[0].dtype)], pieces
    )
    return joined


def gather_rows(rows, stages):
    pieces = [rows]
    for bit, bits in reversed(stages):
        held = join(pieces)
        received = [from_mask(held, r << bit) for r in range(1, 1 << bits)]
        pieces = [held, *received] if bit else [*pieces, *received]
    return pieces


def share_kernel(batch, count, routes, *refs):
    received, residual = refs[:count], refs[count]
    total, message = refs[count + 1 :]
    rows, width = residual.shape[1:]
    value = received[0][...]
    for ref in received[1:]:
        value = value + ref[:, :width].astype(jnp.float32)
    total[:rows, :width] = value[:rows] + residual[batch].astype(jnp.float32)
    total[rows:, :width] = value[rows:]
    message[:, :width] = total[:, :width].astype(jnp.bfloat16)
    base = width // LANES * LANES
    used = width - base
    lane = lax.broadcasted_iota(jnp.int32, (2 * rows, LANES), 1)
    row = lax.broadcasted_iota(jnp.int32, (2 * rows, LANES), 0)
    named = lane < 0
    for i in range(routes.shape[2]):
        for t in range(routes.shape[1]):
            named |= (row == i) & (lane == used + routes[batch, t, i])
    end = jnp.where(lane < used, total[:, base:], jnp.where(named, 1.0, 0.0))
    message[:, base:] = end.astype(jnp.bfloat16)


def norm_kernel(total, mine, theirs, router, attended, payload):
    rows, width = attended.shape
    base = width // LANES * LANES
    used = width - base
    lane = lax.broadcasted_iota(jnp.int32, (2 * rows, LANES), 1)
    place = lax.broadcasted_iota(jnp.int32, (EXPERTS, LANES), 1) - used
    place -= lax.broadcasted_iota(jnp.int32, (EXPERTS, LANES), 0)
    first = jnp.where(place == 0, 1.0, 0.0).astype(jnp.bfloat16)
    second = jnp.where(place == EXPERTS, 1.0, 0.0).astype(jnp.bfloat16)
    other = theirs[...].astype(jnp.float32)
    swapped = jnp.concatenate([other[rows:, :width], other[:rows, :width]], axis=0)
    value = total[:, :width] + swapped
    attended[...] = value[:rows].astype(jnp.bfloat16)
    value = value.astype(jnp.bfloat16).astype(jnp.float32)
    mean = jnp.sum(value * value, axis=1, keepdims=True) * (1.0 / width)
    normed = (value * lax.rsqrt(mean + 1e-05)).astype(jnp.bfloat16)
    payload[:, :width] = normed
    logits = lax.dot_general(normed, router[...], ROWS_LAST, preferred_element_type=jnp.float32)
    ends = jnp.concatenate(
        [mine[:, base:].astype(jnp.float32)[:rows], other[:rows, base:]], axis=0
    )
    named = lax.dot_general(
        ends.astype(jnp.bfloat16), first, ROWS_LAST, preferred_element_type=jnp.float32
    )
    named = named > 0.5
    top = jnp.max(jnp.where(named, logits, -jnp.inf), axis=1, keepdims=True)
    weight = jnp.where(named, jnp.exp(jnp.where(named, logits - top, 0.0)), 0.0)
    gate = weight / jnp.sum(weight, axis=1, keepdims=True)
    high = gate.astype(jnp.bfloat16)
    low = (gate - high.astype(jnp.float32)).astype(jnp.bfloat16)
    end = jnp.dot(high, first, preferred_element_type=jnp.float32)
    end = end + jnp.dot(low, second, preferred_element_type=jnp.float32)
    kept = payload[:, base:].astype(jnp.float32)
    payload[:, base:] = jnp.where(lane < used, kept, end).astype(jnp.bfloat16)


def attend(batch, total, received, residual, routes, router, stages):
    rows, width = residual.shape[1:]
    wide = padded(width)
    total, message = whole_call(
        functools.partial(share_kernel, batch, 1 + len(received)),
        "share",
        [
            jax.ShapeDtypeStruct((2 * rows, wide), jnp.float32),
            jax.ShapeDtypeStruct((2 * rows, wide), jnp.bfloat16),
        ],
        [total, *received, residual],
        scalars=[routes],
        cost_estimate=pl.CostEstimate(flops=60000000000, bytes_accessed=180000000, transcendentals=0),
    )
    theirs = from_mask(message, 1 << stages[-1][0])
    return whole_call(
        norm_kernel,
        "norm",
        [
            jax.ShapeDtypeStruct((rows, width), jnp.bfloat16),
            jax.ShapeDtypeStruct((2 * rows, wide), jnp.bfloat16),
        ],
        [total, message, theirs, router],
    )


def finish_kernel(batch, *refs):
    rows = refs[:batch]
    sums = refs[batch:-2]
    attended, layer = refs[-2:]
    each = rows[0].shape[0]
    begin = 0
    for total, received in zip(sums[::2], sums[1::2]):
        size = total.shape[1]
        some = slice(begin, begin + size)
        value = total[...] + received[:, :size].astype(jnp.float32)
        for m in range(batch):
            mixture = value[m * each : (m + 1) * each]
            layer[m, :, some] = (rows[m][:, some].astype(jnp.float32) + mixture).astype(
                jnp.bfloat16
            )
        begin += size
    for m in range(batch):
        attended[m] = rows[m][...]


def attention_kernel(group, block, lengths, place, far_q, far_kv, far, *refs):
    outs = refs[:group]
    q_ref, kv_ref, near, query, scores, mixed, done = refs[group:]
    small = [
        pltpu.make_async_copy(far_q, q_ref, done.at[0]),
        pltpu.make_async_copy(far_kv, kv_ref, done.at[1]),
    ]
    for copy in small:
        copy.start()
    batch, rows, window, pair = near.shape
    steps = [(m, i) for m in range(batch) for i in range(0, rows, block)]
    size = min(COPY_ROWS, block)
    copies = [
        pltpu.make_async_copy(
            far.at[m, pl.ds(i, size)], near.at[m, pl.ds(i, size)], done.at[index + 2]
        )
        for index, (m, i) in enumerate((m, i) for m in range(batch) for i in range(0, rows, size))
    ]
    started = finished = 0
    low = lax.broadcasted_iota(jnp.int32, (block, pair), 1) < HD
    position = lax.broadcasted_iota(jnp.int32, (QPK, window), 1)
    upper = lax.broadcasted_iota(jnp.int32, (2 * QPK, window), 0) < QPK
    heads = QPK // group
    for m, i in steps:
        while started < min(finished + COPIES_AHEAD, len(copies)):
            copies[started].start()
            started += 1
        some = slice(i, i + block)
        if finished == 0:
            for copy in small:
                copy.wait()
        for h in range(QPK):
            tile = q_ref[m, some, (h // 2) * pair : (h // 2 + 1) * pair].astype(jnp.float32)
            tile = tile * (1.0 / math.sqrt(HD))
            if h % 2:
                tile = pltpu.roll(tile, HD, 1)
            query[pl.ds(h, block, stride=QPK), :] = jnp.where(low, tile, 0.0)
        fresh = kv_ref[m, some, :].astype(jnp.float32)
        fresh = jnp.broadcast_to(fresh[:, None, :], (block, QPK, pair))
        fresh = fresh.reshape(block * QPK, pair)
        own = jnp.sum(query[...] * fresh, axis=1, keepdims=True)
        first = place[0] * rows + i
        for _ in range(block // size):
            copies[finished].wait()
            finished += 1
            if started < len(copies):
                copies[started].start()
                started += 1
        for r in range(0, block, 2):
            part = slice(r * QPK, (r + 2) * QPK)
            found = lax.dot_general(
                query[part, :].astype(jnp.bfloat16),
                near[m, i + r : i + r + 2].reshape(2 * window, pair),
                ROWS_LAST,
                preferred_element_type=jnp.float32,
            )
            for k in (0, 1):
                own_part = found[k * QPK : (k + 1) * QPK, k * window : (k + 1) * window]
                scores[(r + k) * QPK : (r + k + 1) * QPK, :] = jnp.where(
                    position < lengths[m, first + r + k], own_part, -jnp.inf
                )
        top = jnp.maximum(jnp.max(scores[...], axis=1, keepdims=True), own)
        weight = jnp.exp(scores[...] - top)
        weight_own = jnp.exp(own - top)
        total = jnp.sum(weight, axis=1, keepdims=True) + weight_own
        scores[...] = weight / total
        prob_own = (weight_own / total).astype(jnp.bfloat16).astype(jnp.float32)
        for r in range(0, block, 2):
            part = slice(r * QPK, (r + 2) * QPK)
            prob = scores[part, :]
            prob = jnp.concatenate(
                [jnp.where(upper, prob, 0.0), jnp.where(upper, 0.0, prob)], axis=1
            )
            mixed[part, :] = jnp.dot(
                prob.astype(jnp.bfloat16),
                near[m, i + r : i + r + 2].reshape(2 * window, pair),
                preferred_element_type=jnp.float32,
            )
        mixed[...] = mixed[...] + prob_own * fresh
        for r in range(group):
            start = (place[0] ^ r) * heads
            for j in range(0, heads, 2):
                left = pltpu.roll(mixed[pl.ds(start + j, block, stride=QPK), :], HD, 1)
                if heads == 1:
                    outs[r][m, some, :] = left[:, :HD].astype(jnp.bfloat16)
                else:
                    right = mixed[pl.ds(start + j + 1, block, stride=QPK), :]
                    outs[r][m, some, j * HD : (j + 2) * HD] = jnp.where(low, left, right).astype(
                        jnp.bfloat16
                    )


def attention(lengths, place, queries, new_kv, cache, group, block=64):
    batch, rows, window, pair = cache.shape
    block = min(block, rows)
    width = QPK // group * HD
    small = pl.BlockSpec(memory_space=pltpu.SMEM)
    whole = pl.BlockSpec(memory_space=pltpu.VMEM)
    return pl.pallas_call(
        functools.partial(attention_kernel, group, block),
        out_shape=[pltpu.VMEM((batch, rows, width), jnp.bfloat16)] * group,
        in_specs=[small] * 2 + [pl.BlockSpec(memory_space=pl.ANY)] * 3,
        out_specs=[whole] * group,
        scratch_shapes=[
            pltpu.VMEM(queries.shape, jnp.bfloat16),
            pltpu.VMEM(new_kv.shape, jnp.bfloat16),
            pltpu.VMEM(cache.shape, jnp.bfloat16),
            pltpu.VMEM((block * QPK, pair), jnp.float32),
            pltpu.VMEM((block * QPK, window), jnp.float32),
            pltpu.VMEM((block * QPK, pair), jnp.float32),
            pltpu.SemaphoreType.DMA((2 + batch * rows // min(COPY_ROWS, block),)),
        ],
        compiler_params=pltpu.CompilerParams(vmem_limit_bytes=56 << 20),
        cost_estimate=pl.CostEstimate(
            flops=10000000000, bytes_accessed=30000000, transcendentals=0
        ),
        name="attention",
    )(lengths, place, queries, new_kv, cache)


def project_kernel(group, masks, me_ref, *refs):
    held = refs[:group]
    weight, outs, wide, rows = refs[group], refs[group + 1 : -2], *refs[-2:]
    batch, members, width = held[0].shape
    for r in range(group):
        wide[r] = held[r][...].astype(jnp.float32)
    me = me_ref[0]
    per_member = members // REQ_DEV
    for p, mask in enumerate(masks):
        block = me ^ mask
        member = (block // per_member) ^ (me % group)
        start = pl.multiple_of((block % per_member) * REQ_DEV, REQ_DEV)
        for m in range(batch):
            at = (m * len(masks) + p) * REQ_DEV
            rows[at : at + REQ_DEV, :] = wide[member, m, pl.ds(start, REQ_DEV), :]
    half, width = outs[0].shape[0], weight.shape[0]
    found = lax.dot_general(
        rows[...].astype(jnp.bfloat16),
        weight[...],
        ROWS_LAST,
        preferred_element_type=jnp.float32,
    )
    for index, out in enumerate(outs):
        out[:, :width] = found[index * half : (index + 1) * half].astype(out.dtype)


def project(me, held, weight, masks, columns, dtype):
    batch, members, width = held[0].shape
    group = len(held)
    half = len(masks) * REQ_DEV
    return whole_call(
        functools.partial(project_kernel, group, masks),
        "project",
        [jax.ShapeDtypeStruct((half, columns), dtype)] * batch,
        [*held, weight],
        scratch=[
            pltpu.VMEM((group,) + held[0].shape, jnp.float32),
            pltpu.VMEM((batch * half, width), jnp.float32),
        ],
        scalars=[me],
        cost_estimate=pl.CostEstimate(
            flops=600_000_000, bytes_accessed=2_000_000, transcendentals=0
        ),
    )


def expert_kernel(batch, count, hidden, me_ref, *refs):
    pieces = refs[:count]
    w_gate, w_up, w_down = refs[count : count + 3]
    keep, send, active, weights, rows = refs[count + 3 :]
    units, width = w_gate.shape
    at = 0
    for piece in pieces:
        rows[at : at + piece.shape[0], :] = piece[...]
        at += piece.shape[0]
    for start in range(0, units, TILE):
        some = slice(start, min(start + TILE, units))
        gate = lax.dot_general(
            rows[:, :width], w_gate[some, :], ROWS_LAST, preferred_element_type=jnp.float32
        )
        up = lax.dot_general(
            rows[:, :width], w_up[some, :], ROWS_LAST, preferred_element_type=jnp.float32
        )
        active[:, some] = ((up + 1.0) * gate * jax.nn.sigmoid(1.702 * gate)).astype(jnp.bfloat16)
    base = width // LANES * LANES
    tail = rows[:, base:].astype(jnp.float32)
    lane = lax.broadcasted_iota(jnp.int32, tail.shape, 1) - (width - base)
    deep = min(units, SPLIT * hidden)
    for index in range(units // deep):
        expert = (me_ref[0] * units + index * deep) // (SPLIT * hidden)
        picked = (lane == expert) | (lane == expert + EXPERTS)
        weight = jnp.sum(jnp.where(picked, tail, 0.0), axis=1, keepdims=True)
        weights[index] = jnp.broadcast_to(weight, weights.shape[1:])
    down_kernel(batch, hidden, 0, active, weights, w_down, keep, send)


def down_kernel(batch, hidden, begin, active, weights, w_down, keep, send):
    units = w_down.shape[0]
    deep = min(units, SPLIT * hidden)
    half, width = keep.shape
    for start in range(0, width, 2 * TILE):
        some = slice(start, min(start + 2 * TILE, width))
        out = 0.0
        for index in range(units // deep):
            part = slice(index * deep, (index + 1) * deep)
            out = out + weights[index, :, :1] * jnp.dot(
                active[:, part],
                w_down[part, begin + some.start : begin + some.stop],
                preferred_element_type=jnp.float32,
            )
        blocks = half // (batch * REQ_DEV)
        for side, ref in enumerate((keep, send)):
            ordered = []
            for p in range(side * blocks, (side + 1) * blocks):
                for m in range(batch):
                    at = (m * 2 * blocks + p) * REQ_DEV
                    ordered.append(out[at : at + REQ_DEV])
            ref[:, some] = jnp.concatenate(ordered, axis=0).astype(ref.dtype)


def expert_sums(me, batch, pieces, w_gate, w_up, w_down):
    hidden, width = w_down.shape[1:]
    units = w_down.shape[0] * hidden
    count = sum(piece.shape[0] for piece in pieces)
    parts = max(1, units // (SPLIT * hidden))
    first = padded(pl.cdiv(width * 10, 16))

    def halves(columns):
        return [
            jax.ShapeDtypeStruct((count // 2, columns), jnp.float32),
            jax.ShapeDtypeStruct((count // 2, padded(columns)), jnp.bfloat16),
        ]

    down = w_down.reshape(units, width)
    keep, send, active, weights = whole_call(
        functools.partial(expert_kernel, batch, len(pieces), hidden),
        "experts",
        halves(first)
        + [
            jax.ShapeDtypeStruct((count, units), jnp.bfloat16),
            jax.ShapeDtypeStruct((parts, count, LANES), jnp.float32),
        ],
        [
            *pieces,
            w_gate.swapaxes(1, 2).reshape(units, width),
            w_up.swapaxes(1, 2).reshape(units, width),
            down,
        ],
        scratch=[pltpu.VMEM((count, pieces[0].shape[1]), jnp.bfloat16)],
        scalars=[me],
    )
    rest = whole_call(
        functools.partial(down_kernel, batch, hidden, first),
        "down",
        halves(width - first),
        [active, weights, down],
    )
    return [(keep, send), rest]


def shards(queries, new_kv, cache, lengths, residual, o_proj, router, w_gate, w_up, w_down, routes):
    device_count = lax.axis_size("req")
    device_index = lax.axis_index("req")
    stages, masks = plan(device_count)
    group_size = max(1, device_count // KVH)
    batch = residual.shape[0]
    me = device_index.astype(jnp.int32)[None]

    held = attention(lengths, me % group_size, queries, new_kv, cache, group_size)
    held = [held[0]] + [from_mask(held[r], r) for r in range(1, group_size)]
    width, middle = o_proj.shape[1], len(masks) // 2
    sent = project(me, held, o_proj.T, masks[middle:], padded(width), jnp.bfloat16)
    kept = project(me, held, o_proj.T, masks[:middle], width, jnp.float32)
    halves = list(zip(kept, sent))
    attended, pieces = [], []
    for m in range(batch):
        total, received = scatter_sum(halves[m], stages[:-1])
        rows, payload = attend(
            m, total, received, residual, routes.swapaxes(1, 2), router.T, stages
        )
        attended.append(rows)
        pieces += gather_rows(payload, stages[:-1])
    sums = []
    for halves in expert_sums(me, batch, pieces, w_gate, w_up, w_down):
        total, (received,) = scatter_sum(halves, stages)
        sums += [total, received]
    return whole_call(
        functools.partial(finish_kernel, batch),
        "finish",
        [jax.ShapeDtypeStruct(residual.shape, jnp.bfloat16)] * 2,
        [*attended, *sums],
    )


def solution(mesh):
    placed = (
        P(None, ("groups", "req"), None),
        P(None, ("groups", "req"), None),
        P(None, ("groups", "req"), None, None),
        P(None, "groups"),
        P(None, ("groups", "req"), None),
        P("req", None),
        P(),
        P("req", None, None),
        P("req", None, None),
        P("req", None, None),
        P(None, ("groups", "req"), None),
    )
    return jax.shard_map(
        shards,
        mesh=mesh,
        in_specs=placed,
        out_specs=(P(None, ("groups", "req"), None), P(None, ("groups", "req"), None)),
        check_vma=False,
    )
```

```python
import functools
import math

import jax
import jax.numpy as jnp
from jax import lax
from jax.experimental import pallas as pl
from jax.experimental.pallas import tpu as pltpu
from jax.sharding import PartitionSpec as P

HD = 64
KVH = 8
QPK = 8
EXPERTS = 16
SPLIT = 4
REQ_DEV = 8
TILE = 256
LANES = 128
COPY_ROWS = 16
COPIES_AHEAD = 4
LIMIT = 16 << 20
AHEAD = pl.CostEstimate(flops=60_000_000_000, bytes_accessed=150_000_000, transcendentals=0)
ROWS_LAST = (((1,), (1,)), ((), ()))


def plan(device_count):
    bits = device_count.bit_length() - 1
    stages, bit = [(0, 1)], 1
    while bit < bits - 1:
        width = min(2, bits - 1 - bit)
        stages.append((bit, width))
        bit += width
    stages.append((bits - 1, 1))
    masks = [0]
    for bit, width in stages:
        masks = [mask | (r << bit) for mask in masks for r in range(1 << width)]
    return stages, masks


def from_mask(value, mask):
    pairs = [(source, source ^ mask) for source in range(lax.axis_size("req"))]
    return lax.ppermute(value, "req", pairs)


def padded(width):
    return pl.cdiv(width, LANES) * LANES


def whole_call(kernel, name, outs, inputs, scratch=(), scalars=(), **options):
    return pl.pallas_call(
        kernel,
        out_shape=outs,
        in_specs=[pl.BlockSpec(memory_space=pltpu.SMEM)] * len(scalars)
        + [pl.BlockSpec(memory_space=pltpu.VMEM)] * len(inputs),
        out_specs=[pl.BlockSpec(memory_space=pltpu.VMEM)] * len(outs),
        scratch_shapes=list(scratch),
        compiler_params=pltpu.CompilerParams(vmem_limit_bytes=LIMIT),
        name=name,
        **options,
    )(*scalars, *inputs)


def split_kernel(count, pieces, *refs):
    total = refs[0][...]
    width = total.shape[1]
    for ref in refs[1:count]:
        total = total + ref[:, :width].astype(jnp.float32)
    outs = refs[count:]
    size = outs[0].shape[0]
    for index, out in enumerate(outs):
        out[...] = total[index * size : (index + 1) * size].astype(out.dtype)


def add_split(total, received, pieces, chunks=1):
    shape = (total.shape[0] // (pieces * chunks), total.shape[1])
    types = [jnp.float32] + [jnp.bfloat16] * (pieces - 1)
    found = whole_call(
        functools.partial(split_kernel, 1 + len(received), pieces),
        "add_split",
        [jax.ShapeDtypeStruct(shape, dtype) for dtype in types] * chunks,
        [total, *received],
    )
    return [found[c * pieces : (c + 1) * pieces] for c in range(chunks)]


def scatter_sum(pieces, stages):
    for index, (bit, bits) in enumerate(stages):
        received = [from_mask(pieces[r], r << bit) for r in range(1, 1 << bits)]
        if index + 1 < len(stages):
            (pieces,) = add_split(pieces[0], received, 1 << stages[index + 1][1])
    return pieces[0], received


def join_kernel(*refs):
    at = 0
    for ref in refs[:-1]:
        refs[-1][at : at + ref.shape[0], :] = ref[...]
        at += ref.shape[0]


def join(pieces):
    if len(pieces) == 1:
        return pieces[0]
    shape = (sum(piece.shape[0] for piece in pieces), pieces[0].shape[1])
    (joined,) = whole_call(
        join_kernel, "join", [jax.ShapeDtypeStruct(shape, pieces[0].dtype)], pieces
    )
    return joined


def gather_rows(rows, stages):
    pieces = [rows]
    for bit, bits in reversed(stages):
        held = join(pieces)
        received = [from_mask(held, r << bit) for r in range(1, 1 << bits)]
        pieces = [held, *received] if bit else [*pieces, *received]
    return pieces


def share_kernel(batch, count, routes, *refs):
    received, residual = refs[:count], refs[count]
    total, message = refs[count + 1 :]
    rows, width = residual.shape[1:]
    value = received[0][...]
    for ref in received[1:]:
        value = value + ref[:, :width].astype(jnp.float32)
    total[:rows, :width] = value[:rows] + residual[batch].astype(jnp.float32)
    total[rows:, :width] = value[rows:]
    message[:, :width] = total[:, :width].astype(jnp.bfloat16)
    base = width // LANES * LANES
    used = width - base
    lane = lax.broadcasted_iota(jnp.int32, (2 * rows, LANES), 1)
    row = lax.broadcasted_iota(jnp.int32, (2 * rows, LANES), 0)
    named = lane < 0
    for i in range(routes.shape[2]):
        for t in range(routes.shape[1]):
            named |= (row == i) & (lane == used + routes[batch, t, i])
    end = jnp.where(lane < used, total[:, base:], jnp.where(named, 1.0, 0.0))
    message[:, base:] = end.astype(jnp.bfloat16)


def norm_kernel(total, mine, theirs, router, attended, payload):
    rows, width = attended.shape
    base = width // LANES * LANES
    used = width - base
    lane = lax.broadcasted_iota(jnp.int32, (2 * rows, LANES), 1)
    place = lax.broadcasted_iota(jnp.int32, (EXPERTS, LANES), 1) - used
    place -= lax.broadcasted_iota(jnp.int32, (EXPERTS, LANES), 0)
    first = jnp.where(place == 0, 1.0, 0.0).astype(jnp.bfloat16)
    second = jnp.where(place == EXPERTS, 1.0, 0.0).astype(jnp.bfloat16)
    other = theirs[...].astype(jnp.float32)
    swapped = jnp.concatenate([other[rows:, :width], other[:rows, :width]], axis=0)
    value = total[:, :width] + swapped
    attended[...] = value[:rows].astype(jnp.bfloat16)
    value = value.astype(jnp.bfloat16).astype(jnp.float32)
    mean = jnp.sum(value * value, axis=1, keepdims=True) * (1.0 / width)
    normed = (value * lax.rsqrt(mean + 1e-05)).astype(jnp.bfloat16)
    payload[:, :width] = normed
    logits = lax.dot_general(normed, router[...], ROWS_LAST, preferred_element_type=jnp.float32)
    ends = jnp.concatenate(
        [mine[:, base:].astype(jnp.float32)[:rows], other[:rows, base:]], axis=0
    )
    named = lax.dot_general(
        ends.astype(jnp.bfloat16), first, ROWS_LAST, preferred_element_type=jnp.float32
    )
    named = named > 0.5
    top = jnp.max(jnp.where(named, logits, -jnp.inf), axis=1, keepdims=True)
    weight = jnp.where(named, jnp.exp(jnp.where(named, logits - top, 0.0)), 0.0)
    gate = weight / jnp.sum(weight, axis=1, keepdims=True)
    high = gate.astype(jnp.bfloat16)
    low = (gate - high.astype(jnp.float32)).astype(jnp.bfloat16)
    end = jnp.dot(high, first, preferred_element_type=jnp.float32)
    end = end + jnp.dot(low, second, preferred_element_type=jnp.float32)
    kept = payload[:, base:].astype(jnp.float32)
    payload[:, base:] = jnp.where(lane < used, kept, end).astype(jnp.bfloat16)


def attend(batch, total, received, residual, routes, router, stages):
    rows, width = residual.shape[1:]
    wide = padded(width)
    total, message = whole_call(
        functools.partial(share_kernel, batch, 1 + len(received)),
        "share",
        [
            jax.ShapeDtypeStruct((2 * rows, wide), jnp.float32),
            jax.ShapeDtypeStruct((2 * rows, wide), jnp.bfloat16),
        ],
        [total, *received, residual],
        scalars=[routes],
        cost_estimate=pl.CostEstimate(flops=60000000000, bytes_accessed=180000000, transcendentals=0),
    )
    theirs = from_mask(message, 1 << stages[-1][0])
    return whole_call(
        norm_kernel,
        "norm",
        [
            jax.ShapeDtypeStruct((rows, width), jnp.bfloat16),
            jax.ShapeDtypeStruct((2 * rows, wide), jnp.bfloat16),
        ],
        [total, message, theirs, router],
    )


def finish_kernel(batch, *refs):
    rows = refs[:batch]
    sums = refs[batch:-2]
    attended, layer = refs[-2:]
    each = rows[0].shape[0]
    begin = 0
    for total, received in zip(sums[::2], sums[1::2]):
        size = total.shape[1]
        some = slice(begin, begin + size)
        value = total[...] + received[:, :size].astype(jnp.float32)
        for m in range(batch):
            mixture = value[m * each : (m + 1) * each]
            layer[m, :, some] = (rows[m][:, some].astype(jnp.float32) + mixture).astype(
                jnp.bfloat16
            )
        begin += size
    for m in range(batch):
        attended[m] = rows[m][...]


def attention_kernel(group, block, lengths, place, far_q, far_kv, far, *refs):
    outs = refs[:group]
    q_ref, kv_ref, near, query, scores, mixed, done = refs[group:]
    small = [
        pltpu.make_async_copy(far_q, q_ref, done.at[0]),
        pltpu.make_async_copy(far_kv, kv_ref, done.at[1]),
    ]
    for copy in small:
        copy.start()
    batch, rows, window, pair = near.shape
    steps = [(m, i) for m in range(batch) for i in range(0, rows, block)]
    size = min(COPY_ROWS, block)
    copies = [
        pltpu.make_async_copy(
            far.at[m, pl.ds(i, size)], near.at[m, pl.ds(i, size)], done.at[index + 2]
        )
        for index, (m, i) in enumerate((m, i) for m in range(batch) for i in range(0, rows, size))
    ]
    started = finished = 0
    low = lax.broadcasted_iota(jnp.int32, (block, pair), 1) < HD
    position = lax.broadcasted_iota(jnp.int32, (QPK, window), 1)
    upper = lax.broadcasted_iota(jnp.int32, (2 * QPK, window), 0) < QPK
    heads = QPK // group
    for m, i in steps:
        while started < min(finished + COPIES_AHEAD, len(copies)):
            copies[started].start()
            started += 1
        some = slice(i, i + block)
        if finished == 0:
            for copy in small:
                copy.wait()
        for h in range(QPK):
            tile = q_ref[m, some, (h // 2) * pair : (h // 2 + 1) * pair].astype(jnp.float32)
            tile = tile * (1.0 / math.sqrt(HD))
            if h % 2:
                tile = pltpu.roll(tile, HD, 1)
            query[pl.ds(h, block, stride=QPK), :] = jnp.where(low, tile, 0.0)
        fresh = kv_ref[m, some, :].astype(jnp.float32)
        fresh = jnp.broadcast_to(fresh[:, None, :], (block, QPK, pair))
        fresh = fresh.reshape(block * QPK, pair)
        own = jnp.sum(query[...] * fresh, axis=1, keepdims=True)
        first = place[0] * rows + i
        for _ in range(block // size):
            copies[finished].wait()
            finished += 1
            if started < len(copies):
                copies[started].start()
                started += 1
        for r in range(0, block, 2):
            part = slice(r * QPK, (r + 2) * QPK)
            found = lax.dot_general(
                query[part, :].astype(jnp.bfloat16),
                near[m, i + r : i + r + 2].reshape(2 * window, pair),
                ROWS_LAST,
                preferred_element_type=jnp.float32,
            )
            for k in (0, 1):
                own_part = found[k * QPK : (k + 1) * QPK, k * window : (k + 1) * window]
                scores[(r + k) * QPK : (r + k + 1) * QPK, :] = jnp.where(
                    position < lengths[m, first + r + k], own_part, -jnp.inf
                )
        top = jnp.maximum(jnp.max(scores[...], axis=1, keepdims=True), own)
        weight = jnp.exp(scores[...] - top)
        weight_own = jnp.exp(own - top)
        total = jnp.sum(weight, axis=1, keepdims=True) + weight_own
        scores[...] = weight / total
        prob_own = (weight_own / total).astype(jnp.bfloat16).astype(jnp.float32)
        for r in range(0, block, 2):
            part = slice(r * QPK, (r + 2) * QPK)
            prob = scores[part, :]
            prob = jnp.concatenate(
                [jnp.where(upper, prob, 0.0), jnp.where(upper, 0.0, prob)], axis=1
            )
            mixed[part, :] = jnp.dot(
                prob.astype(jnp.bfloat16),
                near[m, i + r : i + r + 2].reshape(2 * window, pair),
                preferred_element_type=jnp.float32,
            )
        mixed[...] = mixed[...] + prob_own * fresh
        for r in range(group):
            start = (place[0] ^ r) * heads
            for j in range(0, heads, 2):
                left = pltpu.roll(mixed[pl.ds(start + j, block, stride=QPK), :], HD, 1)
                if heads == 1:
                    outs[r][m, some, :] = left[:, :HD].astype(jnp.bfloat16)
                else:
                    right = mixed[pl.ds(start + j + 1, block, stride=QPK), :]
                    outs[r][m, some, j * HD : (j + 2) * HD] = jnp.where(low, left, right).astype(
                        jnp.bfloat16
                    )


def attention(lengths, place, queries, new_kv, cache, group, block=64):
    batch, rows, window, pair = cache.shape
    block = min(block, rows)
    width = QPK // group * HD
    small = pl.BlockSpec(memory_space=pltpu.SMEM)
    whole = pl.BlockSpec(memory_space=pltpu.VMEM)
    return pl.pallas_call(
        functools.partial(attention_kernel, group, block),
        out_shape=[pltpu.VMEM((batch, rows, width), jnp.bfloat16)] * group,
        in_specs=[small] * 2 + [pl.BlockSpec(memory_space=pl.ANY)] * 3,
        out_specs=[whole] * group,
        scratch_shapes=[
            pltpu.VMEM(queries.shape, jnp.bfloat16),
            pltpu.VMEM(new_kv.shape, jnp.bfloat16),
            pltpu.VMEM(cache.shape, jnp.bfloat16),
            pltpu.VMEM((block * QPK, pair), jnp.float32),
            pltpu.VMEM((block * QPK, window), jnp.float32),
            pltpu.VMEM((block * QPK, pair), jnp.float32),
            pltpu.SemaphoreType.DMA((2 + batch * rows // min(COPY_ROWS, block),)),
        ],
        compiler_params=pltpu.CompilerParams(vmem_limit_bytes=56 << 20),
        cost_estimate=pl.CostEstimate(
            flops=10000000000, bytes_accessed=30000000, transcendentals=0
        ),
        name="attention",
    )(lengths, place, queries, new_kv, cache)


def project_kernel(group, masks, me_ref, *refs):
    held = refs[:group]
    weight, outs, wide, rows = refs[group], refs[group + 1 : -2], *refs[-2:]
    batch, members, width = held[0].shape
    for r in range(group):
        wide[r] = held[r][...].astype(jnp.float32)
    me = me_ref[0]
    per_member = members // REQ_DEV
    for p, mask in enumerate(masks):
        block = me ^ mask
        member = (block // per_member) ^ (me % group)
        start = pl.multiple_of((block % per_member) * REQ_DEV, REQ_DEV)
        for m in range(batch):
            at = (m * len(masks) + p) * REQ_DEV
            rows[at : at + REQ_DEV, :] = wide[member, m, pl.ds(start, REQ_DEV), :]
    half, width = outs[0].shape[0], weight.shape[0]
    found = lax.dot_general(
        rows[...].astype(jnp.bfloat16),
        weight[...],
        ROWS_LAST,
        preferred_element_type=jnp.float32,
    )
    for index, out in enumerate(outs):
        out[:, :width] = found[index * half : (index + 1) * half].astype(out.dtype)


def project(me, held, weight, masks, columns, dtype):
    batch, members, width = held[0].shape
    group = len(held)
    half = len(masks) * REQ_DEV
    return whole_call(
        functools.partial(project_kernel, group, masks),
        "project",
        [jax.ShapeDtypeStruct((half, columns), dtype)] * batch,
        [*held, weight],
        scratch=[
            pltpu.VMEM((group,) + held[0].shape, jnp.float32),
            pltpu.VMEM((batch * half, width), jnp.float32),
        ],
        scalars=[me],
        cost_estimate=pl.CostEstimate(
            flops=600_000_000, bytes_accessed=2_000_000, transcendentals=0
        ),
    )


def expert_kernel(batch, count, hidden, me_ref, *refs):
    pieces = refs[:count]
    w_gate, w_up, w_down = refs[count : count + 3]
    keep, send, active, weights, rows = refs[count + 3 :]
    units, width = w_gate.shape
    at = 0
    for piece in pieces:
        rows[at : at + piece.shape[0], :] = piece[...]
        at += piece.shape[0]
    for start in range(0, units, TILE):
        some = slice(start, min(start + TILE, units))
        gate = lax.dot_general(
            rows[:, :width], w_gate[some, :], ROWS_LAST, preferred_element_type=jnp.float32
        )
        up = lax.dot_general(
            rows[:, :width], w_up[some, :], ROWS_LAST, preferred_element_type=jnp.float32
        )
        active[:, some] = ((up + 1.0) * gate * jax.nn.sigmoid(1.702 * gate)).astype(jnp.bfloat16)
    base = width // LANES * LANES
    tail = rows[:, base:].astype(jnp.float32)
    lane = lax.broadcasted_iota(jnp.int32, tail.shape, 1) - (width - base)
    deep = min(units, SPLIT * hidden)
    for index in range(units // deep):
        expert = (me_ref[0] * units + index * deep) // (SPLIT * hidden)
        picked = (lane == expert) | (lane == expert + EXPERTS)
        weight = jnp.sum(jnp.where(picked, tail, 0.0), axis=1, keepdims=True)
        weights[index] = jnp.broadcast_to(weight, weights.shape[1:])
    down_kernel(batch, hidden, 0, active, weights, w_down, keep, send)


def down_kernel(batch, hidden, begin, active, weights, w_down, keep, send):
    units = w_down.shape[0]
    deep = min(units, SPLIT * hidden)
    half, width = keep.shape
    for start in range(0, width, 2 * TILE):
        some = slice(start, min(start + 2 * TILE, width))
        out = 0.0
        for index in range(units // deep):
            part = slice(index * deep, (index + 1) * deep)
            out = out + weights[index, :, :1] * jnp.dot(
                active[:, part],
                w_down[part, begin + some.start : begin + some.stop],
                preferred_element_type=jnp.float32,
            )
        blocks = half // (batch * REQ_DEV)
        for side, ref in enumerate((keep, send)):
            ordered = []
            for p in range(side * blocks, (side + 1) * blocks):
                for m in range(batch):
                    at = (m * 2 * blocks + p) * REQ_DEV
                    ordered.append(out[at : at + REQ_DEV])
            ref[:, some] = jnp.concatenate(ordered, axis=0).astype(ref.dtype)


def expert_sums(me, batch, pieces, w_gate, w_up, w_down):
    hidden, width = w_down.shape[1:]
    units = w_down.shape[0] * hidden
    count = sum(piece.shape[0] for piece in pieces)
    parts = max(1, units // (SPLIT * hidden))
    first = padded(pl.cdiv(width * 10, 16))

    def halves(columns):
        return [
            jax.ShapeDtypeStruct((count // 2, columns), jnp.float32),
            jax.ShapeDtypeStruct((count // 2, padded(columns)), jnp.bfloat16),
        ]

    down = w_down.reshape(units, width)
    keep, send, active, weights = whole_call(
        functools.partial(expert_kernel, batch, len(pieces), hidden),
        "experts",
        halves(first)
        + [
            jax.ShapeDtypeStruct((count, units), jnp.bfloat16),
            jax.ShapeDtypeStruct((parts, count, LANES), jnp.float32),
        ],
        [
            *pieces,
            w_gate.swapaxes(1, 2).reshape(units, width),
            w_up.swapaxes(1, 2).reshape(units, width),
            down,
        ],
        scratch=[pltpu.VMEM((count, pieces[0].shape[1]), jnp.bfloat16)],
        scalars=[me],
    )
    rest = whole_call(
        functools.partial(down_kernel, batch, hidden, first),
        "down",
        halves(width - first),
        [active, weights, down],
    )
    return [(keep, send), rest]


def shards(queries, new_kv, cache, lengths, residual, o_proj, router, w_gate, w_up, w_down, routes):
    device_count = lax.axis_size("req")
    device_index = lax.axis_index("req")
    stages, masks = plan(device_count)
    group_size = max(1, device_count // KVH)
    batch = residual.shape[0]
    me = device_index.astype(jnp.int32)[None]

    held = attention(lengths, me % group_size, queries, new_kv, cache, group_size)
    held = [held[0]] + [from_mask(held[r], r) for r in range(1, group_size)]
    width, middle = o_proj.shape[1], len(masks) // 2
    sent = project(me, held, o_proj.T, masks[middle:], padded(width), jnp.bfloat16)
    kept = project(me, held, o_proj.T, masks[:middle], width, jnp.float32)
    halves = list(zip(kept, sent))
    attended, pieces = [], []
    for m in range(batch):
        total, received = scatter_sum(halves[m], stages[:-1])
        rows, payload = attend(
            m, total, received, residual, routes.swapaxes(1, 2), router.T, stages
        )
        attended.append(rows)
        pieces += gather_rows(payload, stages[:-1])
    sums = []
    for halves in expert_sums(me, batch, pieces, w_gate, w_up, w_down):
        total, (received,) = scatter_sum(halves, stages)
        sums += [total, received]
    return whole_call(
        functools.partial(finish_kernel, batch),
        "finish",
        [jax.ShapeDtypeStruct(residual.shape, jnp.bfloat16)] * 2,
        [*attended, *sums],
    )


def solution(mesh):
    placed = (
        P(None, ("groups", "req"), None),
        P(None, ("groups", "req"), None),
        P(None, ("groups", "req"), None, None),
        P(None, "groups"),
        P(None, ("groups", "req"), None),
        P("req", None),
        P(),
        P("req", None, None),
        P("req", None, None),
        P("req", None, None),
        P(None, ("groups", "req"), None),
    )
    return jax.shard_map(
        shards,
        mesh=mesh,
        in_specs=placed,
        out_specs=(P(None, ("groups", "req"), None), P(None, ("groups", "req"), None)),
        check_vma=False,
    )
```
